32 devices in a mesh: tile: 8 (over z, y), shard: 4 (over x, core).
Axes of the slice: x: 2, y: 2, z: 4, core: 2. Of those that a mesh axis runs over, the one named last changes fastest.
Arguments:
- gaussians: float32 [59, 65536], P(None, ('tile', 'shard')), may hold values from -10 to 10, as said below
- camera: float32 [4], replicated, may hold values from -1000 to 1000, as said below
- fetch_index: int32 [32, 2048], P(('tile', 'shard')), may hold values from 0 to 2047, as said below
- tile_ids: int32 [32, 16], P(('tile', 'shard')), may hold values from 0 to 511, as said below
- tile_lists: int32 [32, 16, 256], P(('tile', 'shard')), may hold values from 0 to 2047, as said below
- tile_counts: int32 [32, 16], P(('tile', 'shard')), may hold values from 1 to 256, as said below
- tile_active: int32 [32, 16], P(('tile', 'shard')), may hold values 0 or 1
- target: float32 [3, 512, 256], P(None, ('tile', 'shard')), may hold values from 0 to 1
Outputs:
- image: float32 [3, 512, 256], P(None, ('tile', 'shard'))
- gaussian_grads: float32 [59, 65536], P(None, ('tile', 'shard'))
The draws below stay inside these ranges and needn't reach their ends.
Inputs may be any that keep to these rules, and one draw needn't show every extreme that they name: `fetch_index`: in row d, block s of 64 entries holds distinct indices into owner s's 2048 Gaussians; over all rows every Gaussian of every owner is named exactly once. `tile_ids`: each row is a part of one permutation of the 512 screen tiles. `tile_lists`: on each device every table position 0 to 2047 appears once among the used entries of its tiles' lists, in order of increasing depth of the Gaussian; unused entries are 0. `tile_counts`: on each device the counts sum to 2048, and one tile has exactly 256. `gaussians`: depth (row 2) lies between 2 and 8; the quaternion's w (row 6) lies between 1 and 2; each Gaussian projects near the tile that lists it. `camera`: fx and fy near 8 * 64; the principal point near the image centre.
All inputs are finite; a program needn't handle non-finite values. No bound on the sum of `tile_active` on one device may be relied on, other than what follows from the above.
Results may differ from the reference program's by a relative error of at most 0.0003.
Values sent between devices are 32-bit elements; how exact they have to be, the bound alone decides.
A program may use at most 128 MiB of HBM per device.

```python
import jax
import jax.numpy as jnp
from jax import lax

CAP = 64
TILES_DEV = 16
TILE_SIDE = 16
SPAN = 256
TILES_X = 64
NEED = 2048
G_DEV = 2048
GAUSSIANS = 65536
LIST = 256
TILES = 512
DEVICES = 32


def arrange(key):
    shard_keys = jax.random.split(jax.random.fold_in(key, 101), DEVICES)
    shard_perms = jax.vmap(lambda part_key: jax.random.permutation(part_key, G_DEV))(shard_keys).astype(jnp.int32)
    fetch = shard_perms.reshape(DEVICES, DEVICES, CAP).transpose(1, 0, 2).reshape(DEVICES, NEED)
    rest = NEED - LIST
    base = rest // (TILES_DEV - 1)
    extra = rest % (TILES_DEV - 1)
    swing = jax.random.randint(jax.random.fold_in(key, 102), (DEVICES, (TILES_DEV - 2) // 2), 0, max(base * 5 // 6, 1)).astype(jnp.int32)
    others = jnp.concatenate([base + swing, base - swing, jnp.full((DEVICES, 1), base + extra, jnp.int32)], axis=1)
    counts = jnp.concatenate([jnp.full((DEVICES, 1), LIST, jnp.int32), others], axis=1)
    order_keys = jax.random.split(jax.random.fold_in(key, 103), DEVICES)
    shuffles = jax.vmap(lambda part_key: jax.random.permutation(part_key, TILES_DEV))(order_keys).astype(jnp.int32)
    counts = jnp.take_along_axis(counts, shuffles, axis=1)
    slot_keys = jax.random.split(jax.random.fold_in(key, 104), DEVICES)
    orders = jax.vmap(lambda part_key: jax.random.permutation(part_key, NEED))(slot_keys).astype(jnp.int32)
    starts = jnp.cumsum(counts, axis=1) - counts
    ranks = jnp.arange(LIST, dtype=jnp.int32)
    index = jnp.minimum(starts[:, :, None] + ranks[None, None, :], NEED - 1).reshape(DEVICES, -1)
    lists = jnp.take_along_axis(orders, index, axis=1).reshape(DEVICES, TILES_DEV, LIST)
    lists = jnp.where(ranks[None, None, :] < counts[:, :, None], lists, 0).astype(jnp.int32)
    position = jnp.argsort(orders, axis=1).astype(jnp.int32)
    slot_tile = (jnp.sum((position[:, :, None] >= starts[:, None, :]).astype(jnp.int32), axis=2) - 1).astype(jnp.int32)
    slot_rank = position - jnp.take_along_axis(starts, slot_tile, axis=1)
    screen = jax.random.permutation(jax.random.fold_in(key, 105), TILES).astype(jnp.int32).reshape(DEVICES, TILES_DEV)
    return (fetch, counts, lists, screen, slot_tile, slot_rank, shard_perms)


def lens(key):
    lens_key = jax.random.fold_in(key, 106)
    parts = jax.random.uniform(lens_key, (4,), jnp.float32)
    focal_x = 8.0 * TILES_X * (0.9 + 0.2 * parts[0])
    focal_y = focal_x * (0.95 + 0.1 * parts[1])
    centre_x = 8.0 * TILES_X + 16.0 * parts[2] - 8.0
    centre_y = 8.0 * (TILES // TILES_X) + 16.0 * parts[3] - 8.0
    return jnp.stack([focal_x, focal_y, centre_x, centre_y])


def draw_camera(key, part):
    return lens(key)


def draw_fetch_index(key, part):
    return arrange(key)[0]


def draw_tile_counts(key, part):
    return arrange(key)[1]


def draw_tile_lists(key, part):
    return arrange(key)[2]


def draw_tile_ids(key, part):
    return arrange(key)[3]


def draw_gaussians(key, part):
    fetch, counts, lists, screen, slot_tile, slot_rank, shard_perms = arrange(key)
    camera = lens(key)
    key = jax.random.fold_in(key, 7)
    inverse = jnp.argsort(shard_perms, axis=1).astype(jnp.int32)
    target_dev = inverse // CAP
    slot = jnp.arange(DEVICES, dtype=jnp.int32)[:, None] * CAP + inverse % CAP
    tile_slot = slot_tile[target_dev, slot].reshape(-1)
    rank = slot_rank[target_dev, slot].reshape(-1)
    flat_dev = target_dev.reshape(-1)
    count = counts[flat_dev, tile_slot]
    tile = screen[flat_dev, tile_slot]
    keys = jax.random.split(key, 8)
    total = GAUSSIANS
    jitter = 10.0
    low_sigma, high_sigma = (2.0, 8.0)
    opac = jax.random.uniform(keys[4], (total,), jnp.float32, -6.0, -2.5)
    dc_part = jnp.clip(0.6 * jax.random.normal(keys[5], (3, 1, total), jnp.float32), -2.0, 2.0)
    high_part = jnp.clip(0.25 * jax.random.normal(keys[6], (3, 15, total), jnp.float32), -1.0, 1.0)
    offsets = jax.random.uniform(keys[0], (2, total), jnp.float32, -jitter, jitter)
    pixel_x = (tile % TILES_X * TILE_SIDE).astype(jnp.float32) + 0.5 * TILE_SIDE + offsets[0]
    pixel_y = (tile // TILES_X * TILE_SIDE).astype(jnp.float32) + 0.5 * TILE_SIDE + offsets[1]
    shift = jax.random.uniform(keys[1], (total,), jnp.float32, 0.1, 0.9)
    depth = 2.0 + 6.0 * (rank.astype(jnp.float32) + shift) / count.astype(jnp.float32)
    mean_x = (pixel_x - camera[2]) * depth / camera[0]
    mean_y = (pixel_y - camera[3]) * depth / camera[1]
    sigma_px = jnp.exp(jax.random.uniform(keys[2], (3, total), jnp.float32, jnp.log(low_sigma), jnp.log(high_sigma)))
    log_scale = jnp.log(sigma_px * depth[None, :] / camera[0])
    quat_w = jax.random.uniform(keys[3], (1, total), jnp.float32, 1.0, 2.0)
    quat_rest = jnp.clip(jax.random.normal(keys[7], (3, total), jnp.float32), -2.0, 2.0)
    coeffs = jnp.concatenate([dc_part, high_part], axis=1).reshape(48, total)
    return jnp.concatenate([jnp.stack([mean_x, mean_y, depth]), log_scale, quat_w, quat_rest, opac[None, :], coeffs], axis=0)


def set_ends(result, stream_key, low, top_value):
    extent = result.shape
    place = [jax.random.randint(jax.random.fold_in(stream_key, axis), (), 0, extent[axis]) for axis in range(len(extent))]
    result = result.at[tuple(place)].set(low)
    longest = extent.index(max(extent))
    place[longest] = (place[longest] + 1) % extent[longest]
    return result.at[tuple(place)].set(top_value)


def steps_of(key, dims, cuts, low, largest):
    level = 1.0
    for dim, blocks in cuts:
        steps = jax.random.uniform(jax.random.fold_in(jax.random.fold_in(key, 6), dim), (blocks,), jnp.float32, low / len(cuts), largest / len(cuts))
        level = level * jnp.repeat(jnp.exp(steps), dims[dim] // blocks).reshape((-1,) + (1,) * (len(dims) - 1 - dim))
    return level


def setup_inputs(seed: int = 0) -> dict:
    splits = jax.random.split(jax.random.key(seed), 9)
    return {
        "gaussians": draw_gaussians(jax.random.fold_in(splits[8], 71), 0),
        "camera": draw_camera(jax.random.fold_in(splits[8], 71), 0),
        "fetch_index": draw_fetch_index(jax.random.fold_in(splits[8], 71), 0),
        "tile_ids": draw_tile_ids(jax.random.fold_in(splits[8], 71), 0),
        "tile_lists": draw_tile_lists(jax.random.fold_in(splits[8], 71), 0),
        "tile_counts": draw_tile_counts(jax.random.fold_in(splits[8], 71), 0),
        "tile_active": set_ends((jax.random.randint(splits[6], (DEVICES, TILES_DEV), 0, 8) < 7).astype(jnp.int32), jax.random.fold_in(splits[6], 1), 0, 1),
        "target": jnp.clip(1.0 * jax.random.uniform(splits[7], (3, TILES, TILE_SIDE * TILE_SIDE), jnp.float32) ** steps_of(splits[7], (3, TILES, TILE_SIDE * TILE_SIDE), ((1, 32),), -0.2, 0.2), 0.0, 1.0),
    }


SH_ZERO = 0.28209479177387814
SH_ONE = 0.4886025119029199
SH_TWO = (1.0925484305920792, -1.0925484305920792, 0.31539156525252005, -1.0925484305920792, 0.5462742152960396)
SH_THREE = (-0.5900435899266435, 2.890611442640554, -0.4570457994644658, 0.3731763325901154, -0.4570457994644658, 1.445305721320277, -0.5900435899266435)

def harmonics(dir_x, dir_y, dir_z):
    sq_x, sq_y, sq_z = (dir_x * dir_x, dir_y * dir_y, dir_z * dir_z)
    rows = [SH_ZERO * jnp.ones_like(dir_x), -SH_ONE * dir_y, SH_ONE * dir_z, -SH_ONE * dir_x, SH_TWO[0] * dir_x * dir_y, SH_TWO[1] * dir_y * dir_z, SH_TWO[2] * (2.0 * sq_z - sq_x - sq_y), SH_TWO[3] * dir_x * dir_z, SH_TWO[4] * (sq_x - sq_y), SH_THREE[0] * dir_y * (3.0 * sq_x - sq_y), SH_THREE[1] * dir_x * dir_y * dir_z, SH_THREE[2] * dir_y * (4.0 * sq_z - sq_x - sq_y), SH_THREE[3] * dir_z * (2.0 * sq_z - 3.0 * sq_x - 3.0 * sq_y), SH_THREE[4] * dir_x * (4.0 * sq_z - sq_x - sq_y), SH_THREE[5] * dir_z * (sq_x - sq_y), SH_THREE[6] * dir_x * (sq_x - 3.0 * sq_y)]
    return jnp.stack(rows)

def project(table, camera):
    focal_x, focal_y, centre_x, centre_y = (camera[0], camera[1], camera[2], camera[3])
    mean_x, mean_y, mean_z = (table[0], table[1], table[2])
    spread = jnp.exp(table[3:6])
    quat = table[6:10]
    quat = quat / jnp.sqrt(lax.optimization_barrier(jnp.sum(quat * quat, axis=0)))
    w_part, x_part, y_part, z_part = (quat[0], quat[1], quat[2], quat[3])
    rotate = [[1.0 - 2.0 * (y_part * y_part + z_part * z_part), 2.0 * (x_part * y_part - w_part * z_part), 2.0 * (x_part * z_part + w_part * y_part)], [2.0 * (x_part * y_part + w_part * z_part), 1.0 - 2.0 * (x_part * x_part + z_part * z_part), 2.0 * (y_part * z_part - w_part * x_part)], [2.0 * (x_part * z_part - w_part * y_part), 2.0 * (y_part * z_part + w_part * x_part), 1.0 - 2.0 * (x_part * x_part + y_part * y_part)]]
    scaled = [[rotate[row][col] * spread[col] for col in range(3)] for row in range(3)]
    sigma = [[scaled[row][0] * scaled[col][0] + scaled[row][1] * scaled[col][1] + scaled[row][2] * scaled[col][2] for col in range(3)] for row in range(3)]
    depth_inv = 1.0 / mean_z
    zeros = jnp.zeros_like(mean_z)
    first_row = [focal_x * depth_inv, zeros, -focal_x * mean_x * depth_inv * depth_inv]
    second_row = [zeros, focal_y * depth_inv, -focal_y * mean_y * depth_inv * depth_inv]

    def quadric(left, right):
        total = zeros
        for row in range(3):
            for col in range(3):
                total = total + left[row] * sigma[row][col] * right[col]
        return total
    cov_a = quadric(first_row, first_row) + 0.3
    cov_b = quadric(first_row, second_row)
    cov_c = quadric(second_row, second_row) + 0.3
    determinant = cov_a * cov_c - cov_b * cov_b
    conic_a = cov_c / determinant
    conic_b = -cov_b / determinant
    conic_c = cov_a / determinant
    screen_x = focal_x * mean_x * depth_inv + centre_x
    screen_y = focal_y * mean_y * depth_inv + centre_y
    opacity = jax.nn.sigmoid(table[10])
    radius = jnp.sqrt(mean_x * mean_x + mean_y * mean_y + mean_z * mean_z)
    basis = harmonics(mean_x / radius, mean_y / radius, mean_z / radius)
    coeffs = table[11:59].reshape(3, 16, -1)
    colour = jnp.maximum(lax.optimization_barrier(jnp.sum(coeffs * basis[None], axis=1)) + 0.5, 0.0)
    return jnp.concatenate([jnp.stack([screen_x, screen_y, conic_a, conic_b, conic_c, opacity]), colour], axis=0)

def tile_pass(features, tile, entries, count, live, goal):
    pixels = jnp.arange(TILE_SIDE * TILE_SIDE, dtype=jnp.int32)
    pixel_x = (tile % TILES_X * TILE_SIDE + pixels % TILE_SIDE).astype(jnp.float32) + 0.5
    pixel_y = (tile // TILES_X * TILE_SIDE + pixels // TILE_SIDE).astype(jnp.float32) + 0.5
    length = entries.shape[0]
    blocks = length // SPAN
    picked = features[:, entries].reshape(9, blocks, SPAN).transpose(1, 0, 2)
    keep = ((jnp.arange(length, dtype=jnp.int32) < count) & (live > 0)).astype(jnp.float32).reshape(blocks, SPAN)

    @jax.checkpoint
    def advance(carry, block):
        transmit, colour = carry
        cols, kept = block
        delta_x = pixel_x[None, :] - cols[0][:, None]
        delta_y = pixel_y[None, :] - cols[1][:, None]
        power = -0.5 * (cols[2][:, None] * delta_x * delta_x + cols[4][:, None] * delta_y * delta_y) - cols[3][:, None] * delta_x * delta_y
        alphas = (cols[5] * kept)[:, None] * jnp.exp(power)
        logged = jnp.log1p(-alphas)
        running = jnp.cumsum(logged, axis=0)
        weights = alphas * transmit[None, :] * jnp.exp(running - logged)
        colour = colour + jnp.dot(cols[6:9], weights, precision=lax.Precision.HIGHEST)
        transmit = transmit * jnp.exp(running[-1])
        return ((transmit, colour), None)
    start = (jnp.ones((TILE_SIDE * TILE_SIDE,), jnp.float32), jnp.zeros((3, TILE_SIDE * TILE_SIDE), jnp.float32))
    (transmit, colour), unused = lax.scan(advance, start, (picked, keep))
    residual = colour - goal
    loss = 0.5 * jnp.sum(residual * residual) * (live > 0).astype(jnp.float32)
    return (colour, loss)

def local_step(table, camera, tiles, entries, counts, live, goal):

    def total(values):
        features = project(values, camera)

        def one_tile(pack):
            return tile_pass(features, pack[0], pack[1], pack[2], pack[3], pack[4])
        colours, losses = lax.map(one_tile, (tiles, entries, counts, live, goal.transpose(1, 0, 2)))
        return (jnp.sum(losses), colours)
    loss, pullback, colours = jax.vjp(total, table, has_aux=True)
    grad_table = pullback(jnp.ones_like(loss))[0]
    return (colours.transpose(1, 0, 2), grad_table)

def reference(gaussians, camera, fetch_index, tile_ids, tile_lists, tile_counts, tile_active, target):
    owners = (jnp.arange(NEED, dtype=jnp.int32) // CAP).astype(jnp.int32)

    def visit(device, state):
        image, grads = state
        device = jnp.asarray(device).astype(jnp.int32)
        places = (owners * G_DEV + fetch_index[device]).astype(jnp.int32)
        table = gaussians[:, places]
        first = (device * TILES_DEV).astype(jnp.int32)
        goal = lax.dynamic_slice_in_dim(target, first, TILES_DEV, 1)
        colours, grad_table = local_step(table, camera, tile_ids[device], tile_lists[device], tile_counts[device], tile_active[device], goal)
        image = lax.dynamic_update_slice_in_dim(image, colours, first, 1)
        grads = grads.at[:, places].add(grad_table)
        return (image, grads)
    start = (jnp.zeros((3, TILES, TILE_SIDE * TILE_SIDE), jnp.float32), jnp.zeros_like(gaussians))
    image, grads = lax.fori_loop(0, DEVICES, visit, start)
    return (image, grads)
```

```python
import functools

import jax
import jax.numpy as jnp
import numpy as np
from jax import lax
from jax.experimental import pallas as pl
from jax.experimental.pallas import tpu as pltpu
from jax.sharding import PartitionSpec as P

TILE_SIDE = 16
TILES_X = 64
PIXELS = TILE_SIDE * TILE_SIDE
PACK = 16
UNROLL = 4
CHUNK = 64
NT = (((1,), (1,)), ((), ()))


SH_ZERO = 0.28209479177387814
SH_ONE = 0.4886025119029199
SH_TWO = (
    1.0925484305920792,
    -1.0925484305920792,
    0.31539156525252005,
    -1.0925484305920792,
    0.5462742152960396,
)
SH_THREE = (
    -0.5900435899266435,
    2.890611442640554,
    -0.4570457994644658,
    0.3731763325901154,
    -0.4570457994644658,
    1.445305721320277,
    -0.5900435899266435,
)


def harmonics(dir_x, dir_y, dir_z):
    sq_x, sq_y, sq_z = (dir_x * dir_x, dir_y * dir_y, dir_z * dir_z)
    rows = [
        SH_ZERO * jnp.ones_like(dir_x),
        -SH_ONE * dir_y,
        SH_ONE * dir_z,
        -SH_ONE * dir_x,
        SH_TWO[0] * dir_x * dir_y,
        SH_TWO[1] * dir_y * dir_z,
        SH_TWO[2] * (2.0 * sq_z - sq_x - sq_y),
        SH_TWO[3] * dir_x * dir_z,
        SH_TWO[4] * (sq_x - sq_y),
        SH_THREE[0] * dir_y * (3.0 * sq_x - sq_y),
        SH_THREE[1] * dir_x * dir_y * dir_z,
        SH_THREE[2] * dir_y * (4.0 * sq_z - sq_x - sq_y),
        SH_THREE[3] * dir_z * (2.0 * sq_z - 3.0 * sq_x - 3.0 * sq_y),
        SH_THREE[4] * dir_x * (4.0 * sq_z - sq_x - sq_y),
        SH_THREE[5] * dir_z * (sq_x - sq_y),
        SH_THREE[6] * dir_x * (sq_x - 3.0 * sq_y),
    ]
    return rows


def project(table, camera):
    focal_x, focal_y, centre_x, centre_y = camera
    mean_x, mean_y, mean_z = table[0:3]
    spread = [jnp.exp(value) for value in table[3:6]]
    quat = table[6:10]
    length = jnp.sqrt(
        quat[0] * quat[0] + quat[1] * quat[1] + quat[2] * quat[2] + quat[3] * quat[3]
    )
    inverse = 1.0 / length
    w_part, x_part, y_part, z_part = [value * inverse for value in quat]
    rotate = [
        [
            1.0 - 2.0 * (y_part * y_part + z_part * z_part),
            2.0 * (x_part * y_part - w_part * z_part),
            2.0 * (x_part * z_part + w_part * y_part),
        ],
        [
            2.0 * (x_part * y_part + w_part * z_part),
            1.0 - 2.0 * (x_part * x_part + z_part * z_part),
            2.0 * (y_part * z_part - w_part * x_part),
        ],
        [
            2.0 * (x_part * z_part - w_part * y_part),
            2.0 * (y_part * z_part + w_part * x_part),
            1.0 - 2.0 * (x_part * x_part + y_part * y_part),
        ],
    ]
    scaled = [[rotate[row][col] * spread[col] for col in range(3)] for row in range(3)]
    depth_inv = 1.0 / mean_z
    ratio_x = mean_x * depth_inv
    ratio_y = mean_y * depth_inv
    scale_x = focal_x * depth_inv
    scale_y = focal_y * depth_inv
    top = [scale_x * (scaled[0][col] - ratio_x * scaled[2][col]) for col in range(3)]
    low = [scale_y * (scaled[1][col] - ratio_y * scaled[2][col]) for col in range(3)]
    cov_a = top[0] * top[0] + top[1] * top[1] + top[2] * top[2] + 0.3
    cov_b = top[0] * low[0] + top[1] * low[1] + top[2] * low[2]
    cov_c = low[0] * low[0] + low[1] * low[1] + low[2] * low[2] + 0.3
    det_inv = 1.0 / (cov_a * cov_c - cov_b * cov_b)
    screen_x = focal_x * ratio_x + centre_x
    screen_y = focal_y * ratio_y + centre_y
    opacity = 1.0 / (1.0 + jnp.exp(-table[10]))
    radius_inv = 1.0 / jnp.sqrt(mean_x * mean_x + mean_y * mean_y + mean_z * mean_z)
    basis = harmonics(mean_x * radius_inv, mean_y * radius_inv, mean_z * radius_inv)
    colours = []
    for channel in range(3):
        total = table[11 + 16 * channel] * basis[0]
        for term in range(1, 16):
            total = total + table[11 + 16 * channel + term] * basis[term]
        colours.append(jnp.maximum(total + 0.5, 0.0))
    return [
        screen_x,
        screen_y,
        cov_c * det_inv,
        -cov_b * det_inv,
        cov_a * det_inv,
        opacity,
    ] + colours


def project_kernel(camera_ref, gauss_ref, out_ref):
    camera = [camera_ref[k] for k in range(4)]

    @pl.loop(0, gauss_ref.shape[1] // 8)
    def _(slab):
        rows = pl.ds(pl.multiple_of(slab * 8, 8), 8)
        values = project([gauss_ref[k, rows, :] for k in range(59)], camera)
        u, v, conic_a, conic_b, conic_c, opacity = values[:6]
        sent = [u, v, -0.5 * conic_a, -conic_b, -0.5 * conic_c, opacity] + values[6:]
        for k in range(9):
            out_ref[k, rows, :] = sent[k]
        for k in range(9, PACK):
            out_ref[k, rows, :] = jnp.zeros((8, 128), jnp.float32)


def project_back_kernel(camera_ref, gauss_ref, moment_ref, out_ref):
    camera = [camera_ref[k] for k in range(4)]

    @pl.loop(0, gauss_ref.shape[1] // 8)
    def _(slab):
        rows = pl.ds(pl.multiple_of(slab * 8, 8), 8)
        values, back = jax.vjp(
            lambda *table: project(list(table), camera),
            *[gauss_ref[k, rows, :] for k in range(59)],
        )
        u, v, conic_a, conic_b, conic_c, opacity = values[:6]
        g_0, g_x, g_y, g_xx, g_xy, g_yy = [moment_ref[k, rows, :] for k in range(6)]
        u = u - moment_ref[11, rows, :]
        v = v - moment_ref[12, rows, :]
        s_x = g_x - u * g_0
        s_y = g_y - v * g_0
        s_xx = g_xx - u * (g_x + s_x)
        s_xy = g_xy - u * g_y - v * s_x
        s_yy = g_yy - v * (g_y + s_y)
        given = [
            conic_a * s_x + conic_b * s_y,
            conic_c * s_y + conic_b * s_x,
            -0.5 * s_xx,
            -s_xy,
            -0.5 * s_yy,
            g_0 / opacity,
        ] + [moment_ref[8 + k, rows, :] for k in range(3)]
        grads = back(given)
        for k in range(59):
            out_ref[k, rows, :] = grads[k]


def split(value):
    high = value.astype(jnp.bfloat16)
    return high, (value - high.astype(jnp.float32)).astype(jnp.bfloat16)


def times(left, right):
    return lax.dot_general(left, right, NT, preferred_element_type=jnp.float32)


def render_kernel(
    ids_ref,
    counts_ref,
    active_ref,
    lists_ref,
    feat_ref,
    target_ref,
    pixel_ref,
    mono_ref,
    image_ref,
    out_ref,
    tab,
    gtab,
    rows,
    alphas,
    trans,
    resid,
):
    need = feat_ref.shape[1]
    slots = image_ref.shape[1]
    for block in range(need // 128):
        lanes = slice(block * 128, block * 128 + 128)
        tab[lanes, 0:PACK] = feat_ref[:, lanes].T
    gtab[...] = jnp.zeros_like(gtab)
    resid[...] = jnp.zeros_like(resid)
    sub = lax.broadcasted_iota(jnp.int32, (8, PIXELS), 0)
    sub_col = lax.broadcasted_iota(jnp.int32, (8, 1), 0)
    lane = lax.broadcasted_iota(jnp.int32, (CHUNK, PACK), 1)

    @pl.loop(0, slots)
    def _(slot):
        tile = ids_ref[slot]
        count = jnp.where(active_ref[slot] > 0, counts_ref[slot], 0)
        steps = (count + 8 * UNROLL - 1) // (8 * UNROLL)
        groups = steps * UNROLL
        centre_x = ((tile % TILES_X) * TILE_SIDE + TILE_SIDE // 2).astype(jnp.float32)
        centre_y = ((tile // TILES_X) * TILE_SIDE + TILE_SIDE // 2).astype(jnp.float32)
        pixel_x = jnp.broadcast_to(pixel_ref[0:1, :] + centre_x, (8, PIXELS))
        pixel_y = jnp.broadcast_to(pixel_ref[1:2, :] + centre_y, (8, PIXELS))

        @pl.loop(0, steps)
        def _(step):
            for part in range(UNROLL):
                group = step * UNROLL + part
                first = pl.multiple_of(group * 8, 8)
                picked = [
                    tab[pl.ds(lists_ref[slot, s * groups + group], 1), :] for s in range(8)
                ]
                rows[pl.ds(first, 8), :] = jnp.concatenate(picked, axis=0)

        def forward(step, left):
            for part in range(UNROLL):
                group = step * UNROLL + part
                here = pl.ds(pl.multiple_of(group * 8, 8), 8)
                row = rows[here, :]
                delta_x = pixel_x - row[:, 0:1]
                delta_y = pixel_y - row[:, 1:2]
                power = (
                    delta_x * (row[:, 2:3] * delta_x + row[:, 3:4] * delta_y)
                    + row[:, 4:5] * delta_y * delta_y
                )
                opacity = jnp.where(sub_col * groups + group < count, row[:, 5:6], 0.0)
                alpha = opacity * jnp.exp(power)
                alphas[here, :] = alpha
                trans[here, :] = left
                left = left * (1.0 - alpha)
            return left

        left = lax.fori_loop(0, steps, forward, jnp.ones((8, PIXELS), jnp.float32))
        ahead = jnp.where(sub == 0, 1.0, pltpu.roll(left, 1, 0))
        for shift in (1, 2, 4):
            ahead = ahead * jnp.where(sub < shift, 1.0, pltpu.roll(ahead, shift, 0))

        def composite(step, sums):
            sums = list(sums)
            for part in range(UNROLL):
                group = step * UNROLL + part
                here = pl.ds(pl.multiple_of(group * 8, 8), 8)
                row = rows[here, :]
                weight = alphas[here, :] * trans[here, :]
                for k in range(3):
                    sums[k] = sums[k] + weight * row[:, 6 + k : 7 + k]
            return tuple(sums)

        zero = jnp.zeros((8, PIXELS), jnp.float32)
        sums = lax.fori_loop(0, steps, composite, (zero, zero, zero))
        total = zero
        errors = []
        for k in range(3):
            part = sums[k] * ahead
            colour = jnp.sum(part, axis=0, keepdims=True)
            image_ref[k, pl.ds(slot, 1), :] = colour
            error = colour - target_ref[k, pl.ds(slot, 1), :]
            resid[8 + k : 9 + k, :] = error
            errors.append(jnp.broadcast_to(error, (8, PIXELS)))
            total = total + part * errors[k]
        behind = jnp.where(sub == 7, 0.0, pltpu.roll(total, 7, 0))
        for shift in (1, 2, 4):
            behind = behind + jnp.where(
                sub >= 8 - shift, 0.0, pltpu.roll(behind, 8 - shift, 0)
            )

        def backward(step, later):
            for part in range(UNROLL):
                group = groups - 1 - (step * UNROLL + part)
                here = pl.ds(pl.multiple_of(group * 8, 8), 8)
                row = rows[here, :]
                alpha = alphas[here, :]
                passed = trans[here, :] * ahead
                shade = (
                    row[:, 6:7] * errors[0] + row[:, 7:8] * errors[1] + row[:, 8:9] * errors[2]
                )
                weight = alpha * passed
                given = weight * shade
                alphas[here, :] = weight
                trans[here, :] = given - alpha * later / (1.0 - alpha)
                later = later + given
            return later

        lax.fori_loop(0, steps, backward, behind)

        mono = mono_ref[...].astype(jnp.bfloat16)
        error_high, error_low = split(resid[...])
        centre = jnp.where(lane == 11, centre_x, 0.0) + jnp.where(lane == 12, centre_y, 0.0)

        @pl.loop(0, (groups * 8 + CHUNK - 1) // CHUNK)
        def _(chunk):
            here = pl.ds(pl.multiple_of(chunk * CHUNK, CHUNK), CHUNK)
            power_high, power_low = split(trans[here, :])
            weight_high, weight_low = split(alphas[here, :])
            rows[here, 0:PACK] = (
                times(power_low, mono)
                + times(weight_low, error_high)
                + times(weight_high, error_low)
                + times(power_high, mono)
                + times(weight_high, error_high)
                + centre
            )

        @pl.loop(0, steps)
        def _(step):
            for part in range(UNROLL):
                group = step * UNROLL + part
                block = rows[pl.ds(pl.multiple_of(group * 8, 8), 8), :]
                for s in range(8):
                    rank = s * groups + group
                    place = jnp.where(rank < count, lists_ref[slot, rank], need)
                    gtab[pl.ds(place, 1), :] = block[s : s + 1, :]

    for block in range(need // 128):
        lanes = slice(block * 128, block * 128 + 128)
        out_ref[:, lanes] = gtab[lanes, 0:PACK].T


def render(features, tiles, lists, counts, active, target):
    need = features.shape[1]
    length = -(-lists.shape[1] // CHUNK) * CHUNK
    spot = np.arange(PIXELS)
    local_x = spot % TILE_SIDE + 0.5 - TILE_SIDE // 2
    local_y = spot // TILE_SIDE + 0.5 - TILE_SIDE // 2
    pixel = np.zeros((8, PIXELS), np.float32)
    pixel[0], pixel[1] = local_x, local_y
    mono = np.zeros((PACK, PIXELS), np.float32)
    mono[0] = 1.0
    mono[1], mono[2] = local_x, local_y
    mono[3], mono[4], mono[5] = local_x * local_x, local_x * local_y, local_y * local_y
    smem = pl.BlockSpec(memory_space=pltpu.SMEM)
    vmem = pl.BlockSpec(memory_space=pltpu.VMEM)
    return pl.pallas_call(
        render_kernel,
        out_shape=(
            jax.ShapeDtypeStruct(target.shape, jnp.float32),
            jax.ShapeDtypeStruct((PACK, need), jnp.float32),
        ),
        in_specs=[smem] * 4 + [vmem] * 4,
        out_specs=(vmem, vmem),
        scratch_shapes=[
            pltpu.VMEM((need, 128), jnp.float32),
            pltpu.VMEM((need + 8, 128), jnp.float32),
            pltpu.VMEM((length, 128), jnp.float32),
            pltpu.VMEM((length, PIXELS), jnp.float32),
            pltpu.VMEM((length, PIXELS), jnp.float32),
            pltpu.VMEM((PACK, PIXELS), jnp.float32),
        ],
        compiler_params=pltpu.CompilerParams(vmem_limit_bytes=40 * 1024 * 1024),
        name="render",
    )(tiles, counts, active, lists, features, target, jnp.asarray(pixel), jnp.asarray(mono))


def per_device(
    gaussians, camera, fetch_index, tile_ids, tile_lists, tile_counts, tile_active, target
):
    axes = ("tile", "shard")
    owned = gaussians.shape[1]
    smem = pl.BlockSpec(memory_space=pltpu.SMEM)
    vmem = pl.BlockSpec(memory_space=pltpu.VMEM)
    slabs = gaussians.reshape(59, owned // 128, 128)
    params = pltpu.CompilerParams(vmem_limit_bytes=40 * 1024 * 1024)
    asked = lax.all_to_all(fetch_index[0], axes, split_axis=0, concat_axis=0, tiled=True)
    features = pl.pallas_call(
        project_kernel,
        out_shape=jax.ShapeDtypeStruct((PACK, owned // 128, 128), jnp.float32),
        in_specs=[smem, vmem],
        out_specs=vmem,
        compiler_params=params,
        name="project",
    )(camera, slabs)
    picked = features.reshape(PACK, owned)[:, asked]
    table = lax.all_to_all(picked, axes, split_axis=1, concat_axis=1, tiled=True)
    image, moments = render(
        table, tile_ids[0], tile_lists[0], tile_counts[0], tile_active[0], target
    )
    returned = lax.all_to_all(moments, axes, split_axis=1, concat_axis=1, tiled=True)
    moments = jnp.zeros_like(returned).at[:, asked].set(returned, unique_indices=True)
    grads = pl.pallas_call(
        project_back_kernel,
        out_shape=jax.ShapeDtypeStruct(slabs.shape, jnp.float32),
        in_specs=[smem, vmem, vmem],
        out_specs=vmem,
        compiler_params=params,
        name="project_back",
    )(camera, slabs, moments.reshape(PACK, owned // 128, 128))
    return (image, grads.reshape(gaussians.shape))


def solution(mesh):
    in_specs = (
        P(None, ("tile", "shard")),
        P(),
        P(("tile", "shard"), None),
        P(("tile", "shard"), None),
        P(("tile", "shard"), None, None),
        P(("tile", "shard"), None),
        P(("tile", "shard"), None),
        P(None, ("tile", "shard"), None),
    )
    out_specs = (P(None, ("tile", "shard"), None), P(None, ("tile", "shard")))
    return jax.shard_map(
        per_device, mesh=mesh, in_specs=in_specs, out_specs=out_specs, check_vma=False
    )
```

```python
import functools

import jax
import jax.numpy as jnp
import numpy as np
from jax import lax
from jax.experimental import pallas as pl
from jax.experimental.pallas import tpu as pltpu
from jax.sharding import PartitionSpec as P

TILE_SIDE = 16
TILES_X = 64
PIXELS = TILE_SIDE * TILE_SIDE
PACK = 16
HALF = 64
UNROLL = 4
CHUNK = 64
NT = (((1,), (1,)), ((), ()))
MESH = pl.DeviceIdType.MESH


SH_ZERO = 0.28209479177387814
SH_ONE = 0.4886025119029199
SH_TWO = (
    1.0925484305920792,
    -1.0925484305920792,
    0.31539156525252005,
    -1.0925484305920792,
    0.5462742152960396,
)
SH_THREE = (
    -0.5900435899266435,
    2.890611442640554,
    -0.4570457994644658,
    0.3731763325901154,
    -0.4570457994644658,
    1.445305721320277,
    -0.5900435899266435,
)


def harmonics(dir_x, dir_y, dir_z):
    sq_x, sq_y, sq_z = (dir_x * dir_x, dir_y * dir_y, dir_z * dir_z)
    rows = [
        SH_ZERO * jnp.ones_like(dir_x),
        -SH_ONE * dir_y,
        SH_ONE * dir_z,
        -SH_ONE * dir_x,
        SH_TWO[0] * dir_x * dir_y,
        SH_TWO[1] * dir_y * dir_z,
        SH_TWO[2] * (2.0 * sq_z - sq_x - sq_y),
        SH_TWO[3] * dir_x * dir_z,
        SH_TWO[4] * (sq_x - sq_y),
        SH_THREE[0] * dir_y * (3.0 * sq_x - sq_y),
        SH_THREE[1] * dir_x * dir_y * dir_z,
        SH_THREE[2] * dir_y * (4.0 * sq_z - sq_x - sq_y),
        SH_THREE[3] * dir_z * (2.0 * sq_z - 3.0 * sq_x - 3.0 * sq_y),
        SH_THREE[4] * dir_x * (4.0 * sq_z - sq_x - sq_y),
        SH_THREE[5] * dir_z * (sq_x - sq_y),
        SH_THREE[6] * dir_x * (sq_x - 3.0 * sq_y),
    ]
    return rows


def project(table, camera):
    focal_x, focal_y, centre_x, centre_y = camera
    mean_x, mean_y, mean_z = table[0:3]
    spread = [jnp.exp(value) for value in table[3:6]]
    quat = table[6:10]
    length = jnp.sqrt(
        quat[0] * quat[0] + quat[1] * quat[1] + quat[2] * quat[2] + quat[3] * quat[3]
    )
    inverse = 1.0 / length
    w_part, x_part, y_part, z_part = [value * inverse for value in quat]
    rotate = [
        [
            1.0 - 2.0 * (y_part * y_part + z_part * z_part),
            2.0 * (x_part * y_part - w_part * z_part),
            2.0 * (x_part * z_part + w_part * y_part),
        ],
        [
            2.0 * (x_part * y_part + w_part * z_part),
            1.0 - 2.0 * (x_part * x_part + z_part * z_part),
            2.0 * (y_part * z_part - w_part * x_part),
        ],
        [
            2.0 * (x_part * z_part - w_part * y_part),
            2.0 * (y_part * z_part + w_part * x_part),
            1.0 - 2.0 * (x_part * x_part + y_part * y_part),
        ],
    ]
    scaled = [[rotate[row][col] * spread[col] for col in range(3)] for row in range(3)]
    depth_inv = 1.0 / mean_z
    ratio_x = mean_x * depth_inv
    ratio_y = mean_y * depth_inv
    scale_x = focal_x * depth_inv
    scale_y = focal_y * depth_inv
    top = [scale_x * (scaled[0][col] - ratio_x * scaled[2][col]) for col in range(3)]
    low = [scale_y * (scaled[1][col] - ratio_y * scaled[2][col]) for col in range(3)]
    cov_a = top[0] * top[0] + top[1] * top[1] + top[2] * top[2] + 0.3
    cov_b = top[0] * low[0] + top[1] * low[1] + top[2] * low[2]
    cov_c = low[0] * low[0] + low[1] * low[1] + low[2] * low[2] + 0.3
    det_inv = 1.0 / (cov_a * cov_c - cov_b * cov_b)
    screen_x = focal_x * ratio_x + centre_x
    screen_y = focal_y * ratio_y + centre_y
    opacity = 1.0 / (1.0 + jnp.exp(-table[10]))
    radius_inv = 1.0 / jnp.sqrt(mean_x * mean_x + mean_y * mean_y + mean_z * mean_z)
    basis = harmonics(mean_x * radius_inv, mean_y * radius_inv, mean_z * radius_inv)
    colours = []
    for channel in range(3):
        total = table[11 + 16 * channel] * basis[0]
        for term in range(1, 16):
            total = total + table[11 + 16 * channel + term] * basis[term]
        colours.append(jnp.maximum(total + 0.5, 0.0))
    return [
        screen_x,
        screen_y,
        cov_c * det_inv,
        -cov_b * det_inv,
        cov_a * det_inv,
        opacity,
    ] + colours


def halves(first, second):
    lane = lax.broadcasted_iota(jnp.int32, (8, 128), 1)
    top = jnp.where(lane < HALF, first, pltpu.roll(second, HALF, 1))
    low = jnp.where(lane < HALF, pltpu.roll(first, HALF, 1), second)
    return jnp.concatenate([top, low], axis=0)


def packed(block):
    lane = lax.broadcasted_iota(jnp.int32, (8, 128), 1)
    top, low = block[0:8, :], block[8:16, :]
    first = jnp.where(lane < HALF, top, pltpu.roll(low, HALF, 1))
    second = jnp.where(lane < HALF, pltpu.roll(top, HALF, 1), low)
    return first, second


def offer_kernel(camera_ref, asked_ref, shift_ref, gauss_ref, out_ref, feat, tab, rows):
    camera = [camera_ref[k] for k in range(4)]
    shift = shift_ref[0]
    feat[...] = jnp.zeros_like(feat)

    @pl.loop(0, gauss_ref.shape[1] // 8)
    def _(slab):
        here = pl.ds(pl.multiple_of(slab * 8, 8), 8)
        values = project([gauss_ref[k, here, :] for k in range(59)], camera)
        u, v, conic_a, conic_b, conic_c, opacity = values[:6]
        sent = [u, v, -0.5 * conic_a, -conic_b, -0.5 * conic_c, opacity] + values[6:]
        for r in range(8):
            lanes = pl.ds(pl.multiple_of(slab * 1024 + r * 128, 128), 128)
            for k in range(9):
                feat[k : k + 1, lanes] = sent[k][r : r + 1, :]

    for block in range(tab.shape[0] // 128):
        lanes = slice(block * 128, block * 128 + 128)
        tab[lanes, 0:PACK] = feat[:, lanes].T

    @pl.loop(0, out_ref.shape[0] // 2)
    def _(pair):
        for half in range(2):
            for k in range(HALF):
                place = asked_ref[2 * pair + half, shift + k]
                rows[half * HALF + k : half * HALF + k + 1, :] = tab[pl.ds(place, 1), :]
        first, second = packed(rows[:, 0:PACK].T)
        out_ref[2 * pair] = first
        out_ref[2 * pair + 1] = second


def settle_kernel(camera_ref, asked_ref, shift_ref, gauss_ref, moment_ref, out_ref, tab, rows, sums):
    camera = [camera_ref[k] for k in range(4)]
    shift = shift_ref[0]

    @pl.loop(0, moment_ref.shape[0] // 2)
    def _(pair):
        rows[:, 0:PACK] = halves(moment_ref[2 * pair], moment_ref[2 * pair + 1]).T
        for half in range(2):
            for k in range(HALF):
                place = asked_ref[2 * pair + half, shift + k]
                tab[pl.ds(place, 1), :] = rows[half * HALF + k : half * HALF + k + 1, :]

    for block in range(tab.shape[0] // 128):
        lanes = slice(block * 128, block * 128 + 128)
        sums[:, lanes] = tab[lanes, 0:PACK].T

    @pl.loop(0, gauss_ref.shape[1] // 8)
    def _(slab):
        here = pl.ds(pl.multiple_of(slab * 8, 8), 8)

        def moment(k):
            parts = [
                sums[k : k + 1, pl.ds(pl.multiple_of(slab * 1024 + r * 128, 128), 128)]
                for r in range(8)
            ]
            return jnp.concatenate(parts, axis=0)

        values, back = jax.vjp(
            lambda *table: project(list(table), camera),
            *[gauss_ref[k, here, :] for k in range(59)],
        )
        u, v, conic_a, conic_b, conic_c, opacity = values[:6]
        g_0, g_x, g_y, g_xx, g_xy, g_yy = [moment(k) for k in range(6)]
        u = u - moment(11)
        v = v - moment(12)
        s_x = g_x - u * g_0
        s_y = g_y - v * g_0
        s_xx = g_xx - u * (g_x + s_x)
        s_xy = g_xy - u * g_y - v * s_x
        s_yy = g_yy - v * (g_y + s_y)
        given = [
            conic_a * s_x + conic_b * s_y,
            conic_c * s_y + conic_b * s_x,
            -0.5 * s_xx,
            -s_xy,
            -0.5 * s_yy,
            g_0 / opacity,
        ] + [moment(8 + k) for k in range(3)]
        grads = back(given)
        for k in range(59):
            out_ref[k, here, :] = grads[k]


def exchange_kernel(sizes, in_ref, out_ref, send_sem, recv_sem, own_sem):
    n = sizes[0] * sizes[1]
    share = n // in_ref.shape[0]
    me = lax.axis_index("tile") * sizes[1] + lax.axis_index("shard")
    barrier = pltpu.get_barrier_semaphore()

    def greet(step, unused):
        peer = lax.rem(me + step, n)
        pl.semaphore_signal(
            barrier,
            inc=1,
            device_id=(peer // sizes[1], lax.rem(peer, sizes[1])),
            device_id_type=MESH,
        )
        return unused

    def transfer(step):
        peer = lax.rem(me + step, n)
        return pltpu.make_async_remote_copy(
            src_ref=in_ref.at[peer // share],
            dst_ref=out_ref.at[me],
            send_sem=send_sem.at[step],
            recv_sem=recv_sem.at[step],
            device_id=(peer // sizes[1], lax.rem(peer, sizes[1])),
            device_id_type=MESH,
        )

    def start(step, unused):
        transfer(step).start()
        return unused

    def finish(step, unused):
        transfer(step).wait()
        return unused

    own = pltpu.make_async_copy(in_ref.at[me // share], out_ref.at[me], own_sem)
    own.start()
    lax.fori_loop(1, n, greet, 0)
    pl.semaphore_wait(barrier, n - 1)
    lax.fori_loop(1, n, start, 0)
    lax.fori_loop(1, n, finish, 0)
    own.wait()


def exchange(blocks, sizes, number, name):
    n = sizes[0] * sizes[1]
    return pl.pallas_call(
        functools.partial(exchange_kernel, sizes),
        out_shape=jax.ShapeDtypeStruct((n,) + blocks.shape[1:], blocks.dtype),
        in_specs=[pl.BlockSpec(memory_space=pltpu.VMEM)],
        out_specs=pl.BlockSpec(memory_space=pltpu.VMEM),
        scratch_shapes=[
            pltpu.SemaphoreType.DMA((n,)),
            pltpu.SemaphoreType.DMA((n,)),
            pltpu.SemaphoreType.DMA,
        ],
        compiler_params=pltpu.CompilerParams(collective_id=number, has_side_effects=True),
        name=name,
    )(blocks)


def split(value):
    high = value.astype(jnp.bfloat16)
    return high, (value - high.astype(jnp.float32)).astype(jnp.bfloat16)


def times(left, right):
    return lax.dot_general(left, right, NT, preferred_element_type=jnp.float32)


def render_kernel(
    ids_ref,
    counts_ref,
    active_ref,
    lists_ref,
    feat_ref,
    target_ref,
    pixel_ref,
    mono_ref,
    image_ref,
    out_ref,
    tab,
    gtab,
    rows,
    alphas,
    trans,
    resid,
):
    need = feat_ref.shape[0] * HALF
    slots = image_ref.shape[1]
    for block in range(need // 128):
        lanes = slice(block * 128, block * 128 + 128)
        tab[lanes, 0:PACK] = halves(feat_ref[2 * block], feat_ref[2 * block + 1]).T
    gtab[...] = jnp.zeros_like(gtab)
    resid[...] = jnp.zeros_like(resid)
    sub = lax.broadcasted_iota(jnp.int32, (8, PIXELS), 0)
    sub_col = lax.broadcasted_iota(jnp.int32, (8, 1), 0)
    lane = lax.broadcasted_iota(jnp.int32, (CHUNK, PACK), 1)

    @pl.loop(0, slots)
    def _(slot):
        tile = ids_ref[slot]
        count = jnp.where(active_ref[slot] > 0, counts_ref[slot], 0)
        steps = (count + 8 * UNROLL - 1) // (8 * UNROLL)
        groups = steps * UNROLL
        centre_x = ((tile % TILES_X) * TILE_SIDE + TILE_SIDE // 2).astype(jnp.float32)
        centre_y = ((tile // TILES_X) * TILE_SIDE + TILE_SIDE // 2).astype(jnp.float32)
        pixel_x = jnp.broadcast_to(pixel_ref[0:1, :] + centre_x, (8, PIXELS))
        pixel_y = jnp.broadcast_to(pixel_ref[1:2, :] + centre_y, (8, PIXELS))

        @pl.loop(0, steps)
        def _(step):
            for part in range(UNROLL):
                group = step * UNROLL + part
                first = pl.multiple_of(group * 8, 8)
                picked = [
                    tab[pl.ds(lists_ref[slot, s * groups + group], 1), :] for s in range(8)
                ]
                rows[pl.ds(first, 8), :] = jnp.concatenate(picked, axis=0)

        def forward(step, left):
            for part in range(UNROLL):
                group = step * UNROLL + part
                here = pl.ds(pl.multiple_of(group * 8, 8), 8)
                row = rows[here, :]
                delta_x = pixel_x - row[:, 0:1]
                delta_y = pixel_y - row[:, 1:2]
                power = (
                    delta_x * (row[:, 2:3] * delta_x + row[:, 3:4] * delta_y)
                    + row[:, 4:5] * delta_y * delta_y
                )
                opacity = jnp.where(sub_col * groups + group < count, row[:, 5:6], 0.0)
                alpha = opacity * jnp.exp(power)
                alphas[here, :] = alpha
                trans[here, :] = left
                left = left * (1.0 - alpha)
            return left

        left = lax.fori_loop(0, steps, forward, jnp.ones((8, PIXELS), jnp.float32))
        ahead = jnp.where(sub == 0, 1.0, pltpu.roll(left, 1, 0))
        for shift in (1, 2, 4):
            ahead = ahead * jnp.where(sub < shift, 1.0, pltpu.roll(ahead, shift, 0))

        def composite(step, sums):
            sums = list(sums)
            for part in range(UNROLL):
                group = step * UNROLL + part
                here = pl.ds(pl.multiple_of(group * 8, 8), 8)
                row = rows[here, :]
                weight = alphas[here, :] * trans[here, :]
                for k in range(3):
                    sums[k] = sums[k] + weight * row[:, 6 + k : 7 + k]
            return tuple(sums)

        zero = jnp.zeros((8, PIXELS), jnp.float32)
        sums = lax.fori_loop(0, steps, composite, (zero, zero, zero))
        total = zero
        errors = []
        for k in range(3):
            part = sums[k] * ahead
            colour = jnp.sum(part, axis=0, keepdims=True)
            image_ref[k, pl.ds(slot, 1), :] = colour
            error = colour - target_ref[k, pl.ds(slot, 1), :]
            resid[8 + k : 9 + k, :] = error
            errors.append(jnp.broadcast_to(error, (8, PIXELS)))
            total = total + part * errors[k]
        behind = jnp.where(sub == 7, 0.0, pltpu.roll(total, 7, 0))
        for shift in (1, 2, 4):
            behind = behind + jnp.where(
                sub >= 8 - shift, 0.0, pltpu.roll(behind, 8 - shift, 0)
            )

        def backward(step, later):
            for part in range(UNROLL):
                group = groups - 1 - (step * UNROLL + part)
                here = pl.ds(pl.multiple_of(group * 8, 8), 8)
                row = rows[here, :]
                alpha = alphas[here, :]
                passed = trans[here, :] * ahead
                shade = (
                    row[:, 6:7] * errors[0] + row[:, 7:8] * errors[1] + row[:, 8:9] * errors[2]
                )
                weight = alpha * passed
                given = weight * shade
                alphas[here, :] = weight
                trans[here, :] = given - alpha * later / (1.0 - alpha)
                later = later + given
            return later

        lax.fori_loop(0, steps, backward, behind)

        mono = mono_ref[...].astype(jnp.bfloat16)
        error_high, error_low = split(resid[...])
        centre = jnp.where(lane == 11, centre_x, 0.0) + jnp.where(lane == 12, centre_y, 0.0)

        @pl.loop(0, (groups * 8 + CHUNK - 1) // CHUNK)
        def _(chunk):
            here = pl.ds(pl.multiple_of(chunk * CHUNK, CHUNK), CHUNK)
            power_high, power_low = split(trans[here, :])
            weight_high, weight_low = split(alphas[here, :])
            rows[here, 0:PACK] = (
                times(power_low, mono)
                + times(weight_low, error_high)
                + times(weight_high, error_low)
                + times(power_high, mono)
                + times(weight_high, error_high)
                + centre
            )

        @pl.loop(0, steps)
        def _(step):
            for part in range(UNROLL):
                group = step * UNROLL + part
                block = rows[pl.ds(pl.multiple_of(group * 8, 8), 8), :]
                for s in range(8):
                    rank = s * groups + group
                    place = jnp.where(rank < count, lists_ref[slot, rank], need)
                    gtab[pl.ds(place, 1), :] = block[s : s + 1, :]

    for block in range(need // 128):
        lanes = slice(block * 128, block * 128 + 128)
        first, second = packed(gtab[lanes, 0:PACK].T)
        out_ref[2 * block] = first
        out_ref[2 * block + 1] = second


def render(features, tiles, lists, counts, active, target):
    need = features.shape[0] * HALF
    length = -(-lists.shape[1] // CHUNK) * CHUNK
    spot = np.arange(PIXELS)
    local_x = spot % TILE_SIDE + 0.5 - TILE_SIDE // 2
    local_y = spot // TILE_SIDE + 0.5 - TILE_SIDE // 2
    pixel = np.zeros((8, PIXELS), np.float32)
    pixel[0], pixel[1] = local_x, local_y
    mono = np.zeros((PACK, PIXELS), np.float32)
    mono[0] = 1.0
    mono[1], mono[2] = local_x, local_y
    mono[3], mono[4], mono[5] = local_x * local_x, local_x * local_y, local_y * local_y
    smem = pl.BlockSpec(memory_space=pltpu.SMEM)
    vmem = pl.BlockSpec(memory_space=pltpu.VMEM)
    return pl.pallas_call(
        render_kernel,
        out_shape=(
            jax.ShapeDtypeStruct(target.shape, jnp.float32),
            jax.ShapeDtypeStruct(features.shape, jnp.float32),
        ),
        in_specs=[smem] * 4 + [vmem] * 4,
        out_specs=(vmem, vmem),
        scratch_shapes=[
            pltpu.VMEM((need, 128), jnp.float32),
            pltpu.VMEM((need + 8, 128), jnp.float32),
            pltpu.VMEM((length, 128), jnp.float32),
            pltpu.VMEM((length, PIXELS), jnp.float32),
            pltpu.VMEM((length, PIXELS), jnp.float32),
            pltpu.VMEM((PACK, PIXELS), jnp.float32),
        ],
        compiler_params=pltpu.CompilerParams(vmem_limit_bytes=40 * 1024 * 1024),
        name="render",
    )(tiles, counts, active, lists, features, target, jnp.asarray(pixel), jnp.asarray(mono))


def per_device(
    sizes,
    gaussians,
    camera,
    fetch_index,
    tile_ids,
    tile_lists,
    tile_counts,
    tile_active,
    target,
):
    owned = gaussians.shape[1]
    need = fetch_index.shape[1]
    n = sizes[0] * sizes[1]
    if need != n * HALF or owned % 1024 != 0:
        raise ValueError("unsupported sizes")
    smem = pl.BlockSpec(memory_space=pltpu.SMEM)
    vmem = pl.BlockSpec(memory_space=pltpu.VMEM)
    slabs = gaussians.reshape(59, owned // 128, 128)
    params = pltpu.CompilerParams(vmem_limit_bytes=40 * 1024 * 1024)
    me = lax.axis_index("tile") * sizes[1] + lax.axis_index("shard")
    shift = (lax.rem(me, 2) * HALF).astype(jnp.int32).reshape(1)
    asked = exchange(fetch_index.reshape(n // 2, 1, 128), sizes, 0, "ask").reshape(n, 128)
    offered = pl.pallas_call(
        offer_kernel,
        out_shape=jax.ShapeDtypeStruct((n, 8, 128), jnp.float32),
        in_specs=[smem, smem, smem, vmem],
        out_specs=vmem,
        scratch_shapes=[
            pltpu.VMEM((PACK, owned), jnp.float32),
            pltpu.VMEM((owned, 128), jnp.float32),
            pltpu.VMEM((128, 128), jnp.float32),
        ],
        compiler_params=params,
        name="offer",
    )(camera, asked, shift, slabs)
    table = exchange(offered, sizes, 1, "fetch")
    image, moments = render(
        table, tile_ids[0], tile_lists[0], tile_counts[0], tile_active[0], target
    )
    returned = exchange(moments, sizes, 2, "give")
    grads = pl.pallas_call(
        settle_kernel,
        out_shape=jax.ShapeDtypeStruct(slabs.shape, jnp.float32),
        in_specs=[smem, smem, smem, vmem, vmem],
        out_specs=vmem,
        scratch_shapes=[
            pltpu.VMEM((owned, 128), jnp.float32),
            pltpu.VMEM((128, 128), jnp.float32),
            pltpu.VMEM((PACK, owned), jnp.float32),
        ],
        compiler_params=params,
        name="settle",
    )(camera, asked, shift, slabs, returned)
    return (image, grads.reshape(gaussians.shape))


def solution(mesh):
    in_specs = (
        P(None, ("tile", "shard")),
        P(),
        P(("tile", "shard"), None),
        P(("tile", "shard"), None),
        P(("tile", "shard"), None, None),
        P(("tile", "shard"), None),
        P(("tile", "shard"), None),
        P(None, ("tile", "shard"), None),
    )
    out_specs = (P(None, ("tile", "shard"), None), P(None, ("tile", "shard")))
    sizes = (mesh.shape["tile"], mesh.shape["shard"])
    return jax.shard_map(
        functools.partial(per_device, sizes), mesh=mesh, in_specs=in_specs, out_specs=out_specs, check_vma=False
    )
```

```python
import functools

import jax
import jax.numpy as jnp
import numpy as np
from jax import lax
from jax.experimental import pallas as pl
from jax.experimental.pallas import tpu as pltpu
from jax.sharding import PartitionSpec as P

TILE_SIDE = 16
TILES_X = 64
PIXELS = TILE_SIDE * TILE_SIDE
PACK = 16
HALF = 64
WIDE = 64
SEGMENTS = 16
STEPS = 8
CHUNK = 256
NN = (((1,), (0,)), ((), ()))
NT = (((1,), (1,)), ((), ()))
MESH = pl.DeviceIdType.MESH


SH_ZERO = 0.28209479177387814
SH_ONE = 0.4886025119029199
SH_TWO = (
    1.0925484305920792,
    -1.0925484305920792,
    0.31539156525252005,
    -1.0925484305920792,
    0.5462742152960396,
)
SH_THREE = (
    -0.5900435899266435,
    2.890611442640554,
    -0.4570457994644658,
    0.3731763325901154,
    -0.4570457994644658,
    1.445305721320277,
    -0.5900435899266435,
)


def harmonics(dir_x, dir_y, dir_z):
    sq_x, sq_y, sq_z = (dir_x * dir_x, dir_y * dir_y, dir_z * dir_z)
    rows = [
        SH_ZERO * jnp.ones_like(dir_x),
        -SH_ONE * dir_y,
        SH_ONE * dir_z,
        -SH_ONE * dir_x,
        SH_TWO[0] * dir_x * dir_y,
        SH_TWO[1] * dir_y * dir_z,
        SH_TWO[2] * (2.0 * sq_z - sq_x - sq_y),
        SH_TWO[3] * dir_x * dir_z,
        SH_TWO[4] * (sq_x - sq_y),
        SH_THREE[0] * dir_y * (3.0 * sq_x - sq_y),
        SH_THREE[1] * dir_x * dir_y * dir_z,
        SH_THREE[2] * dir_y * (4.0 * sq_z - sq_x - sq_y),
        SH_THREE[3] * dir_z * (2.0 * sq_z - 3.0 * sq_x - 3.0 * sq_y),
        SH_THREE[4] * dir_x * (4.0 * sq_z - sq_x - sq_y),
        SH_THREE[5] * dir_z * (sq_x - sq_y),
        SH_THREE[6] * dir_x * (sq_x - 3.0 * sq_y),
    ]
    return rows


def project(table, camera):
    focal_x, focal_y, centre_x, centre_y = camera
    mean_x, mean_y, mean_z = table[0:3]
    spread = [jnp.exp(value) for value in table[3:6]]
    quat = table[6:10]
    length = jnp.sqrt(
        quat[0] * quat[0] + quat[1] * quat[1] + quat[2] * quat[2] + quat[3] * quat[3]
    )
    inverse = 1.0 / length
    w_part, x_part, y_part, z_part = [value * inverse for value in quat]
    rotate = [
        [
            1.0 - 2.0 * (y_part * y_part + z_part * z_part),
            2.0 * (x_part * y_part - w_part * z_part),
            2.0 * (x_part * z_part + w_part * y_part),
        ],
        [
            2.0 * (x_part * y_part + w_part * z_part),
            1.0 - 2.0 * (x_part * x_part + z_part * z_part),
            2.0 * (y_part * z_part - w_part * x_part),
        ],
        [
            2.0 * (x_part * z_part - w_part * y_part),
            2.0 * (y_part * z_part + w_part * x_part),
            1.0 - 2.0 * (x_part * x_part + y_part * y_part),
        ],
    ]
    scaled = [[rotate[row][col] * spread[col] for col in range(3)] for row in range(3)]
    depth_inv = 1.0 / mean_z
    ratio_x = mean_x * depth_inv
    ratio_y = mean_y * depth_inv
    scale_x = focal_x * depth_inv
    scale_y = focal_y * depth_inv
    top = [scale_x * (scaled[0][col] - ratio_x * scaled[2][col]) for col in range(3)]
    low = [scale_y * (scaled[1][col] - ratio_y * scaled[2][col]) for col in range(3)]
    cov_a = top[0] * top[0] + top[1] * top[1] + top[2] * top[2] + 0.3
    cov_b = top[0] * low[0] + top[1] * low[1] + top[2] * low[2]
    cov_c = low[0] * low[0] + low[1] * low[1] + low[2] * low[2] + 0.3
    det_inv = 1.0 / (cov_a * cov_c - cov_b * cov_b)
    screen_x = focal_x * ratio_x + centre_x
    screen_y = focal_y * ratio_y + centre_y
    opacity = 1.0 / (1.0 + jnp.exp(-table[10]))
    radius_inv = 1.0 / jnp.sqrt(mean_x * mean_x + mean_y * mean_y + mean_z * mean_z)
    basis = harmonics(mean_x * radius_inv, mean_y * radius_inv, mean_z * radius_inv)
    colours = []
    for channel in range(3):
        total = table[11 + 16 * channel] * basis[0]
        for term in range(1, 16):
            total = total + table[11 + 16 * channel + term] * basis[term]
        colours.append(jnp.maximum(total + 0.5, 0.0))
    return [
        screen_x,
        screen_y,
        cov_c * det_inv,
        -cov_b * det_inv,
        cov_a * det_inv,
        opacity,
    ] + colours


def halves(first, second):
    lane = lax.broadcasted_iota(jnp.int32, (8, 128), 1)
    top = jnp.where(lane < HALF, first, pltpu.roll(second, HALF, 1))
    low = jnp.where(lane < HALF, pltpu.roll(first, HALF, 1), second)
    return jnp.concatenate([top, low], axis=0)


def packed(block):
    lane = lax.broadcasted_iota(jnp.int32, (8, 128), 1)
    top, low = block[0:8, :], block[8:16, :]
    first = jnp.where(lane < HALF, top, pltpu.roll(low, HALF, 1))
    second = jnp.where(lane < HALF, pltpu.roll(top, HALF, 1), low)
    return first, second


def offer_kernel(camera_ref, asked_ref, shift_ref, gauss_ref, out_ref, feat, tab, rows):
    camera = [camera_ref[k] for k in range(4)]
    shift = shift_ref[0]
    feat[...] = jnp.zeros_like(feat)

    @pl.loop(0, gauss_ref.shape[1] // 8)
    def _(slab):
        here = pl.ds(pl.multiple_of(slab * 8, 8), 8)
        values = project([gauss_ref[k, here, :] for k in range(59)], camera)
        u, v, conic_a, conic_b, conic_c, opacity = values[:6]
        sent = [u, v, -0.5 * conic_a, -conic_b, -0.5 * conic_c, opacity] + values[6:]
        for r in range(8):
            lanes = pl.ds(pl.multiple_of(slab * 1024 + r * 128, 128), 128)
            for k in range(9):
                feat[k : k + 1, lanes] = sent[k][r : r + 1, :]

    for block in range(tab.shape[0] // 128):
        lanes = slice(block * 128, block * 128 + 128)
        tab[lanes, 0:PACK] = feat[:, lanes].T

    @pl.loop(0, out_ref.shape[0] // 2)
    def _(pair):
        for half in range(2):
            for k in range(HALF):
                place = asked_ref[2 * pair + half, shift + k]
                rows[half * HALF + k : half * HALF + k + 1, :] = tab[pl.ds(place, 1), :]
        first, second = packed(rows[:, 0:PACK].T)
        out_ref[2 * pair] = first
        out_ref[2 * pair + 1] = second


def settle_kernel(camera_ref, asked_ref, shift_ref, gauss_ref, moment_ref, out_ref, tab, rows, sums):
    camera = [camera_ref[k] for k in range(4)]
    shift = shift_ref[0]

    @pl.loop(0, moment_ref.shape[0] // 2)
    def _(pair):
        rows[:, 0:PACK] = halves(moment_ref[2 * pair], moment_ref[2 * pair + 1]).T
        for half in range(2):
            for k in range(HALF):
                place = asked_ref[2 * pair + half, shift + k]
                tab[pl.ds(place, 1), :] = rows[half * HALF + k : half * HALF + k + 1, :]

    for block in range(tab.shape[0] // 128):
        lanes = slice(block * 128, block * 128 + 128)
        sums[:, lanes] = tab[lanes, 0:PACK].T

    @pl.loop(0, gauss_ref.shape[1] // 8)
    def _(slab):
        here = pl.ds(pl.multiple_of(slab * 8, 8), 8)

        def moment(k):
            parts = [
                sums[k : k + 1, pl.ds(pl.multiple_of(slab * 1024 + r * 128, 128), 128)]
                for r in range(8)
            ]
            return jnp.concatenate(parts, axis=0)

        values, back = jax.vjp(
            lambda *table: project(list(table), camera),
            *[gauss_ref[k, here, :] for k in range(59)],
        )
        u, v, conic_a, conic_b, conic_c, opacity = values[:6]
        g_0, g_x, g_y, g_xx, g_xy, g_yy = [moment(k) for k in range(6)]
        u = u - moment(11)
        v = v - moment(12)
        s_x = g_x - u * g_0
        s_y = g_y - v * g_0
        s_xx = g_xx - u * (g_x + s_x)
        s_xy = g_xy - u * g_y - v * s_x
        s_yy = g_yy - v * (g_y + s_y)
        given = [
            conic_a * s_x + conic_b * s_y,
            conic_c * s_y + conic_b * s_x,
            -0.5 * s_xx,
            -s_xy,
            -0.5 * s_yy,
            g_0 / opacity,
        ] + [moment(8 + k) for k in range(3)]
        grads = back(given)
        for k in range(59):
            out_ref[k, here, :] = grads[k]


def exchange_kernel(sizes, in_ref, out_ref, send_sem, recv_sem, own_sem):
    n = sizes[0] * sizes[1]
    share = n // in_ref.shape[0]
    me = lax.axis_index("tile") * sizes[1] + lax.axis_index("shard")
    barrier = pltpu.get_barrier_semaphore()

    def greet(step, unused):
        peer = lax.rem(me + step, n)
        pl.semaphore_signal(
            barrier,
            inc=1,
            device_id=(peer // sizes[1], lax.rem(peer, sizes[1])),
            device_id_type=MESH,
        )
        return unused

    def transfer(step):
        peer = lax.rem(me + step, n)
        return pltpu.make_async_remote_copy(
            src_ref=in_ref.at[peer // share],
            dst_ref=out_ref.at[me],
            send_sem=send_sem.at[step],
            recv_sem=recv_sem.at[step],
            device_id=(peer // sizes[1], lax.rem(peer, sizes[1])),
            device_id_type=MESH,
        )

    def start(step, unused):
        transfer(step).start()
        return unused

    def finish(step, unused):
        transfer(step).wait()
        return unused

    own = pltpu.make_async_copy(in_ref.at[me // share], out_ref.at[me], own_sem)
    own.start()
    lax.fori_loop(1, n, greet, 0)
    pl.semaphore_wait(barrier, n - 1)
    lax.fori_loop(1, n, start, 0)
    lax.fori_loop(1, n, finish, 0)
    own.wait()


def exchange(blocks, sizes, number, name):
    n = sizes[0] * sizes[1]
    return pl.pallas_call(
        functools.partial(exchange_kernel, sizes),
        out_shape=jax.ShapeDtypeStruct((n,) + blocks.shape[1:], blocks.dtype),
        in_specs=[pl.BlockSpec(memory_space=pltpu.VMEM)],
        out_specs=pl.BlockSpec(memory_space=pltpu.VMEM),
        scratch_shapes=[
            pltpu.SemaphoreType.DMA((n,)),
            pltpu.SemaphoreType.DMA((n,)),
            pltpu.SemaphoreType.DMA,
        ],
        compiler_params=pltpu.CompilerParams(collective_id=number, has_side_effects=True),
        name=name,
    )(blocks)


def split(value):
    high = value.astype(jnp.bfloat16)
    return high, (value - high.astype(jnp.float32)).astype(jnp.bfloat16)


def times(left, right, dims):
    return lax.dot_general(left, right, dims, preferred_element_type=jnp.float32)


def render_kernel(
    ids_ref,
    counts_ref,
    active_ref,
    lists_ref,
    feat_ref,
    target_ref,
    pixel_ref,
    mono_ref,
    image_ref,
    out_ref,
    tab,
    rows,
    alphas,
    weights,
    powers,
    errors,
):
    need = feat_ref.shape[0] * HALF
    span = need // SEGMENTS
    slots = image_ref.shape[1]
    lane = lax.broadcasted_iota(jnp.int32, (1, 128), 1)

    for block in range(need // 128):
        lanes = slice(block * 128, block * 128 + 128)
        values = halves(feat_ref[2 * block], feat_ref[2 * block + 1])
        colours = [jnp.broadcast_to(values[6 + k : 7 + k, :], (16, 128)) for k in range(3)]
        tab[lanes, 0:WIDE] = jnp.concatenate([values] + colours, axis=0).T

    def centre(slot):
        tile = ids_ref[slot]
        centre_x = ((tile % TILES_X) * TILE_SIDE + TILE_SIDE // 2).astype(jnp.float32)
        centre_y = ((tile // TILES_X) * TILE_SIDE + TILE_SIDE // 2).astype(jnp.float32)
        return centre_x, centre_y

    def of_tile(slot):
        return (lane >= 16) & (lane < WIDE) & (lane % 16 == slot)

    def places(slot, start, step):
        for part in range(8):
            rank = step * 8 + part
            entry = start + rank
            used = rank < counts_ref[slot]
            row = jnp.where(used, (entry % span) * SEGMENTS + entry // span, need)
            yield used, lists_ref[slot, rank], row

    def pick(slot, start):
        count = counts_ref[slot]
        centre_x, centre_y = centre(slot)
        alive = jnp.where(active_ref[slot] > 0, 1.0, 0.0)
        scale = jnp.where((lane < 5) | of_tile(slot), 1.0, jnp.where(lane == 5, alive, 0.0))
        offset = jnp.where(lane == 0, -centre_x, jnp.where(lane == 1, -centre_y, 0.0))
        offset = jnp.where(lane == 6, start.astype(jnp.float32), offset)
        offset = jnp.where(lane == 7, (start + count).astype(jnp.float32), offset)

        @pl.loop(0, (count + 7) // 8)
        def _(step):
            for used, place, row in places(slot, start, step):
                rows[pl.ds(row, 1), :] = tab[pl.ds(place, 1), :] * scale + offset

        return start + count

    lax.fori_loop(0, slots, pick, jnp.int32(0))

    pixel_x = jnp.broadcast_to(pixel_ref[0:1, :], (8, PIXELS))
    pixel_y = jnp.broadcast_to(pixel_ref[1:2, :], (8, PIXELS))
    sets = range(SEGMENTS // 8)
    sub = lax.broadcasted_iota(jnp.int32, (8, 1), 0)
    bases = [((sub + 8 * q) * span).astype(jnp.float32) for q in sets]
    one = jnp.ones((8, PIXELS), jnp.float32)
    zero = jnp.zeros((8, PIXELS), jnp.float32)

    def forward(step, state):
        left, seen = list(state[0]), list(state[1])
        for part in range(STEPS):
            place = step * STEPS + part
            for q in sets:
                here = pl.ds(pl.multiple_of(place * SEGMENTS + 8 * q, 8), 8)
                row = rows[here, :]
                delta_x = pixel_x - row[:, 0:1]
                delta_y = pixel_y - row[:, 1:2]
                power = (
                    delta_x * (row[:, 2:3] * delta_x + row[:, 3:4] * delta_y)
                    + row[:, 4:5] * delta_y * delta_y
                )
                alpha = row[:, 5:6] * jnp.exp(power)
                begins = jnp.where(row[:, 6:7] == bases[q] + place.astype(jnp.float32), 1.0, 0.0)
                seen[q] = jnp.maximum(seen[q], begins)
                passed = jnp.where(jnp.broadcast_to(begins, (8, PIXELS)) > 0.0, 1.0, left[q])
                alphas[here, :] = alpha
                weights[here, :] = alpha * passed
                left[q] = passed * (1.0 - alpha)
        return tuple(left), tuple(seen)

    none = jnp.zeros((8, 1), jnp.float32)
    left, seen = lax.fori_loop(
        0, span // STEPS, forward, (tuple(one for q in sets), tuple(none for q in sets))
    )
    carry = one[0:1, :]
    ahead = []
    for q in sets:
        parts = []
        for k in range(8):
            parts.append(carry)
            begun = seen[q][k : k + 1, :]
            carry = left[q][k : k + 1, :] * (begun + (1.0 - begun) * carry)
        ahead.append(jnp.concatenate(parts, axis=0))

    def composite(chunk, image):
        here = pl.ds(pl.multiple_of(chunk * CHUNK, CHUNK), CHUNK)
        for group in range(CHUNK // 8):
            q = group % len(sets)
            part = pl.ds(pl.multiple_of(chunk * CHUNK + 8 * group, 8), 8)
            head = jnp.where(rows[part, 6:7] < bases[q], 1.0, 0.0)
            factor = jnp.where(jnp.broadcast_to(head, (8, PIXELS)) > 0.0, ahead[q], 1.0)
            weights[part, :] = weights[part, :] * factor
        colour_high, colour_low = split(rows[here, 0:WIDE].T)
        weight_high, weight_low = split(weights[here, :])
        return (
            image
            + times(colour_low, weight_high, NN)
            + times(colour_high, weight_low, NN)
            + times(colour_high, weight_high, NN)
        )

    chunks = need // CHUNK
    image = lax.fori_loop(0, chunks, composite, jnp.zeros((WIDE, PIXELS), jnp.float32))
    errors[0:16, :] = jnp.zeros((16, PIXELS), jnp.float32)
    for k in range(3):
        part = image[16 + 16 * k : 32 + 16 * k, :]
        image_ref[k] = part
        errors[16 + 16 * k : 32 + 16 * k, :] = part - target_ref[k]

    def backward(step, later):
        later = list(later)
        chunk = chunks - 1 - step
        here = pl.ds(pl.multiple_of(chunk * CHUNK, CHUNK), CHUNK)
        colour_high, colour_low = split(rows[here, 0:WIDE])
        error_high, error_low = split(errors[...])
        powers[here, :] = (
            times(colour_low, error_high, NN)
            + times(colour_high, error_low, NN)
            + times(colour_high, error_high, NN)
        )
        for group in reversed(range(CHUNK // 8)):
            q = group % len(sets)
            part = pl.ds(pl.multiple_of(chunk * CHUNK + 8 * group, 8), 8)
            after = (chunk * (CHUNK // SEGMENTS) + group // len(sets) + 1).astype(jnp.float32)
            ends = jnp.where(rows[part, 7:8] == bases[q] + after, 1.0, 0.0)
            alpha = alphas[part, :]
            given = weights[part, :] * powers[part, :]
            rest = jnp.where(jnp.broadcast_to(ends, (8, PIXELS)) > 0.0, 0.0, later[q])
            ratio = alpha / (1.0 - alpha)
            alphas[part, :] = ratio
            powers[part, :] = given - ratio * rest
            later[q] = rest + given
        return tuple(later)

    later = lax.fori_loop(0, chunks, backward, tuple(zero for q in sets))
    carry = zero[0:1, :]
    behind = []
    for q in reversed(sets):
        final = pl.ds((span - 1) * SEGMENTS + 8 * q, 8)
        onward = jnp.where(rows[final, 7:8] > bases[q] + span, 1.0, 0.0) * (1.0 - seen[q])
        parts = []
        for k in reversed(range(8)):
            parts.append(carry)
            carry = later[q][k : k + 1, :] + onward[k : k + 1, :] * carry
        behind.append(jnp.concatenate(parts[::-1], axis=0))
    behind = behind[::-1]

    @pl.loop(0, chunks)
    def _(chunk):
        here = pl.ds(pl.multiple_of(chunk * CHUNK, CHUNK), CHUNK)
        for group in range(CHUNK // 8):
            q = group % len(sets)
            part = pl.ds(pl.multiple_of(chunk * CHUNK + 8 * group, 8), 8)
            tail = jnp.where(rows[part, 7:8] > bases[q] + span, 1.0, 0.0)
            rest = jnp.where(jnp.broadcast_to(tail, (8, PIXELS)) > 0.0, behind[q], 0.0)
            powers[part, :] = powers[part, :] - alphas[part, :] * rest
        power_high, power_low = split(powers[here, :])
        weight_high, weight_low = split(weights[here, :])
        error_high, error_low = split(errors[...])
        mono = mono_ref[...].astype(jnp.bfloat16)
        rows[here, 0:WIDE] = (
            times(power_low, mono, NT)
            + times(weight_low, error_high, NT)
            + times(weight_high, error_low, NT)
            + times(power_high, mono, NT)
            + times(weight_high, error_high, NT)
        )

    def put(slot, start):
        count = counts_ref[slot]
        centre_x, centre_y = centre(slot)
        scale = jnp.where((lane < 6) | of_tile(slot), 1.0, 0.0)
        offset = jnp.where(lane == 11, centre_x, jnp.where(lane == 12, centre_y, 0.0))

        @pl.loop(0, (count + 7) // 8)
        def _(step):
            for used, place, row in places(slot, start, step):
                spot = jnp.where(used, place, need)
                tab[pl.ds(spot, 1), :] = rows[pl.ds(row, 1), :] * scale + offset

        return start + count

    lax.fori_loop(0, slots, put, jnp.int32(0))
    sub = lax.broadcasted_iota(jnp.int32, (8, 128), 0)
    for block in range(need // 128):
        lanes = slice(block * 128, block * 128 + 128)
        values = tab[lanes, 0:WIDE].T
        low = values[8:16, :]
        for k in range(3):
            summed = jnp.sum(values[16 + 16 * k : 32 + 16 * k, :], axis=0, keepdims=True)
            low = jnp.where(sub == k, summed, low)
        first, second = packed(jnp.concatenate([values[0:8, :], low], axis=0))
        out_ref[2 * block] = first
        out_ref[2 * block + 1] = second


def render(features, tiles, lists, counts, active, target):
    need = features.shape[0] * HALF
    if target.shape[1] != 16 or need % (SEGMENTS * 128) != 0:
        raise ValueError("unsupported sizes")
    spot = np.arange(PIXELS)
    local_x = spot % TILE_SIDE + 0.5 - TILE_SIDE // 2
    local_y = spot // TILE_SIDE + 0.5 - TILE_SIDE // 2
    pixel = np.zeros((8, PIXELS), np.float32)
    pixel[0], pixel[1] = local_x, local_y
    mono = np.zeros((WIDE, PIXELS), np.float32)
    mono[0] = 1.0
    mono[1], mono[2] = local_x, local_y
    mono[3], mono[4], mono[5] = local_x * local_x, local_x * local_y, local_y * local_y
    smem = pl.BlockSpec(memory_space=pltpu.SMEM)
    vmem = pl.BlockSpec(memory_space=pltpu.VMEM)
    return pl.pallas_call(
        render_kernel,
        out_shape=(
            jax.ShapeDtypeStruct(target.shape, jnp.float32),
            jax.ShapeDtypeStruct(features.shape, jnp.float32),
        ),
        in_specs=[smem] * 4 + [vmem] * 4,
        out_specs=(vmem, vmem),
        scratch_shapes=[
            pltpu.VMEM((need + 8, 128), jnp.float32),
            pltpu.VMEM((need + 8, 128), jnp.float32),
            pltpu.VMEM((need, PIXELS), jnp.float32),
            pltpu.VMEM((need, PIXELS), jnp.float32),
            pltpu.VMEM((need, PIXELS), jnp.float32),
            pltpu.VMEM((WIDE, PIXELS), jnp.float32),
        ],
        compiler_params=pltpu.CompilerParams(vmem_limit_bytes=48 * 1024 * 1024),
        name="render",
    )(tiles, counts, active, lists, features, target, jnp.asarray(pixel), jnp.asarray(mono))


def per_device(
    sizes,
    gaussians,
    camera,
    fetch_index,
    tile_ids,
    tile_lists,
    tile_counts,
    tile_active,
    target,
):
    owned = gaussians.shape[1]
    need = fetch_index.shape[1]
    n = sizes[0] * sizes[1]
    if need != n * HALF or owned % 1024 != 0:
        raise ValueError("unsupported sizes")
    smem = pl.BlockSpec(memory_space=pltpu.SMEM)
    vmem = pl.BlockSpec(memory_space=pltpu.VMEM)
    slabs = gaussians.reshape(59, owned // 128, 128)
    params = pltpu.CompilerParams(vmem_limit_bytes=40 * 1024 * 1024)
    me = lax.axis_index("tile") * sizes[1] + lax.axis_index("shard")
    shift = (lax.rem(me, 2) * HALF).astype(jnp.int32).reshape(1)
    asked = exchange(fetch_index.reshape(n // 2, 1, 128), sizes, 0, "ask").reshape(n, 128)
    offered = pl.pallas_call(
        offer_kernel,
        out_shape=jax.ShapeDtypeStruct((n, 8, 128), jnp.float32),
        in_specs=[smem, smem, smem, vmem],
        out_specs=vmem,
        scratch_shapes=[
            pltpu.VMEM((PACK, owned), jnp.float32),
            pltpu.VMEM((owned, 128), jnp.float32),
            pltpu.VMEM((128, 128), jnp.float32),
        ],
        compiler_params=params,
        name="offer",
    )(camera, asked, shift, slabs)
    table = exchange(offered, sizes, 1, "fetch")
    image, moments = render(
        table, tile_ids[0], tile_lists[0], tile_counts[0], tile_active[0], target
    )
    returned = exchange(moments, sizes, 2, "give")
    grads = pl.pallas_call(
        settle_kernel,
        out_shape=jax.ShapeDtypeStruct(slabs.shape, jnp.float32),
        in_specs=[smem, smem, smem, vmem, vmem],
        out_specs=vmem,
        scratch_shapes=[
            pltpu.VMEM((owned, 128), jnp.float32),
            pltpu.VMEM((128, 128), jnp.float32),
            pltpu.VMEM((PACK, owned), jnp.float32),
        ],
        compiler_params=params,
        name="settle",
    )(camera, asked, shift, slabs, returned)
    return (image, grads.reshape(gaussians.shape))


def solution(mesh):
    in_specs = (
        P(None, ("tile", "shard")),
        P(),
        P(("tile", "shard"), None),
        P(("tile", "shard"), None),
        P(("tile", "shard"), None, None),
        P(("tile", "shard"), None),
        P(("tile", "shard"), None),
        P(None, ("tile", "shard"), None),
    )
    out_specs = (P(None, ("tile", "shard"), None), P(None, ("tile", "shard")))
    sizes = (mesh.shape["tile"], mesh.shape["shard"])
    return jax.shard_map(
        functools.partial(per_device, sizes), mesh=mesh, in_specs=in_specs, out_specs=out_specs, check_vma=False
    )
```

```python
import functools

import jax
import jax.numpy as jnp
import numpy as np
from jax import lax
from jax.experimental import pallas as pl
from jax.experimental.pallas import tpu as pltpu
from jax.sharding import PartitionSpec as P

TILE_SIDE = 16
TILES_X = 64
PIXELS = TILE_SIDE * TILE_SIDE
PACK = 16
HALF = 64
WIDE = 64
SEGMENTS = 16
STEPS = 8
BATCH = 16
CHUNK = 256
NN = (((1,), (0,)), ((), ()))
NT = (((1,), (1,)), ((), ()))
MESH = pl.DeviceIdType.MESH


SH_ZERO = 0.28209479177387814
SH_ONE = 0.4886025119029199
SH_TWO = (
    1.0925484305920792,
    -1.0925484305920792,
    0.31539156525252005,
    -1.0925484305920792,
    0.5462742152960396,
)
SH_THREE = (
    -0.5900435899266435,
    2.890611442640554,
    -0.4570457994644658,
    0.3731763325901154,
    -0.4570457994644658,
    1.445305721320277,
    -0.5900435899266435,
)


def harmonics(dir_x, dir_y, dir_z):
    sq_x, sq_y, sq_z = (dir_x * dir_x, dir_y * dir_y, dir_z * dir_z)
    rows = [
        SH_ZERO * jnp.ones_like(dir_x),
        -SH_ONE * dir_y,
        SH_ONE * dir_z,
        -SH_ONE * dir_x,
        SH_TWO[0] * dir_x * dir_y,
        SH_TWO[1] * dir_y * dir_z,
        SH_TWO[2] * (2.0 * sq_z - sq_x - sq_y),
        SH_TWO[3] * dir_x * dir_z,
        SH_TWO[4] * (sq_x - sq_y),
        SH_THREE[0] * dir_y * (3.0 * sq_x - sq_y),
        SH_THREE[1] * dir_x * dir_y * dir_z,
        SH_THREE[2] * dir_y * (4.0 * sq_z - sq_x - sq_y),
        SH_THREE[3] * dir_z * (2.0 * sq_z - 3.0 * sq_x - 3.0 * sq_y),
        SH_THREE[4] * dir_x * (4.0 * sq_z - sq_x - sq_y),
        SH_THREE[5] * dir_z * (sq_x - sq_y),
        SH_THREE[6] * dir_x * (sq_x - 3.0 * sq_y),
    ]
    return rows


def project(table, camera):
    focal_x, focal_y, centre_x, centre_y = camera
    mean_x, mean_y, mean_z = table[0:3]
    spread = [jnp.exp(value) for value in table[3:6]]
    quat = table[6:10]
    length = jnp.sqrt(
        quat[0] * quat[0] + quat[1] * quat[1] + quat[2] * quat[2] + quat[3] * quat[3]
    )
    inverse = 1.0 / length
    w_part, x_part, y_part, z_part = [value * inverse for value in quat]
    rotate = [
        [
            1.0 - 2.0 * (y_part * y_part + z_part * z_part),
            2.0 * (x_part * y_part - w_part * z_part),
            2.0 * (x_part * z_part + w_part * y_part),
        ],
        [
            2.0 * (x_part * y_part + w_part * z_part),
            1.0 - 2.0 * (x_part * x_part + z_part * z_part),
            2.0 * (y_part * z_part - w_part * x_part),
        ],
        [
            2.0 * (x_part * z_part - w_part * y_part),
            2.0 * (y_part * z_part + w_part * x_part),
            1.0 - 2.0 * (x_part * x_part + y_part * y_part),
        ],
    ]
    scaled = [[rotate[row][col] * spread[col] for col in range(3)] for row in range(3)]
    depth_inv = 1.0 / mean_z
    ratio_x = mean_x * depth_inv
    ratio_y = mean_y * depth_inv
    scale_x = focal_x * depth_inv
    scale_y = focal_y * depth_inv
    top = [scale_x * (scaled[0][col] - ratio_x * scaled[2][col]) for col in range(3)]
    low = [scale_y * (scaled[1][col] - ratio_y * scaled[2][col]) for col in range(3)]
    cov_a = top[0] * top[0] + top[1] * top[1] + top[2] * top[2] + 0.3
    cov_b = top[0] * low[0] + top[1] * low[1] + top[2] * low[2]
    cov_c = low[0] * low[0] + low[1] * low[1] + low[2] * low[2] + 0.3
    det_inv = 1.0 / (cov_a * cov_c - cov_b * cov_b)
    screen_x = focal_x * ratio_x + centre_x
    screen_y = focal_y * ratio_y + centre_y
    opacity = 1.0 / (1.0 + jnp.exp(-table[10]))
    radius_inv = 1.0 / jnp.sqrt(mean_x * mean_x + mean_y * mean_y + mean_z * mean_z)
    basis = harmonics(mean_x * radius_inv, mean_y * radius_inv, mean_z * radius_inv)
    colours = []
    for channel in range(3):
        total = table[11 + 16 * channel] * basis[0]
        for term in range(1, 16):
            total = total + table[11 + 16 * channel + term] * basis[term]
        colours.append(jnp.maximum(total + 0.5, 0.0))
    return [
        screen_x,
        screen_y,
        cov_c * det_inv,
        -cov_b * det_inv,
        cov_a * det_inv,
        opacity,
    ] + colours


def halves(first, second):
    lane = lax.broadcasted_iota(jnp.int32, (8, 128), 1)
    top = jnp.where(lane < HALF, first, pltpu.roll(second, HALF, 1))
    low = jnp.where(lane < HALF, pltpu.roll(first, HALF, 1), second)
    return jnp.concatenate([top, low], axis=0)


def packed(block):
    lane = lax.broadcasted_iota(jnp.int32, (8, 128), 1)
    top, low = block[0:8, :], block[8:16, :]
    first = jnp.where(lane < HALF, top, pltpu.roll(low, HALF, 1))
    second = jnp.where(lane < HALF, pltpu.roll(top, HALF, 1), low)
    return first, second


def offer_kernel(camera_ref, asked_ref, shift_ref, gauss_ref, out_ref, feat, tab, rows):
    camera = [camera_ref[k] for k in range(4)]
    shift = shift_ref[0]
    feat[...] = jnp.zeros_like(feat)

    @pl.loop(0, gauss_ref.shape[1] // 8)
    def _(slab):
        here = pl.ds(pl.multiple_of(slab * 8, 8), 8)
        values = project([gauss_ref[k, here, :] for k in range(59)], camera)
        u, v, conic_a, conic_b, conic_c, opacity = values[:6]
        sent = [u, v, -0.5 * conic_a, -conic_b, -0.5 * conic_c, opacity] + values[6:]
        for r in range(8):
            lanes = pl.ds(pl.multiple_of(slab * 1024 + r * 128, 128), 128)
            for k in range(9):
                feat[k : k + 1, lanes] = sent[k][r : r + 1, :]

    for block in range(tab.shape[0] // 128):
        lanes = slice(block * 128, block * 128 + 128)
        tab[lanes, 0:PACK] = feat[:, lanes].T

    @pl.loop(0, out_ref.shape[0] // 2)
    def _(pair):
        for half in range(2):
            for k in range(0, HALF, BATCH):
                picked = [
                    tab[pl.ds(asked_ref[2 * pair + half, shift + k + part], 1), :]
                    for part in range(BATCH)
                ]
                first = half * HALF + k
                rows[first : first + BATCH, :] = jnp.concatenate(picked, axis=0)
        first, second = packed(rows[:, 0:PACK].T)
        out_ref[2 * pair] = first
        out_ref[2 * pair + 1] = second


def settle_kernel(camera_ref, asked_ref, shift_ref, gauss_ref, moment_ref, out_ref, tab, rows, sums):
    camera = [camera_ref[k] for k in range(4)]
    shift = shift_ref[0]

    @pl.loop(0, moment_ref.shape[0] // 2)
    def _(pair):
        rows[:, 0:PACK] = halves(moment_ref[2 * pair], moment_ref[2 * pair + 1]).T
        for half in range(2):
            for k in range(0, HALF, BATCH):
                first = half * HALF + k
                block = rows[first : first + BATCH, :]
                for part in range(BATCH):
                    place = asked_ref[2 * pair + half, shift + k + part]
                    tab[pl.ds(place, 1), :] = block[part : part + 1, :]

    for block in range(tab.shape[0] // 128):
        lanes = slice(block * 128, block * 128 + 128)
        sums[:, lanes] = tab[lanes, 0:PACK].T

    @pl.loop(0, gauss_ref.shape[1] // 8)
    def _(slab):
        here = pl.ds(pl.multiple_of(slab * 8, 8), 8)

        def moment(k):
            parts = [
                sums[k : k + 1, pl.ds(pl.multiple_of(slab * 1024 + r * 128, 128), 128)]
                for r in range(8)
            ]
            return jnp.concatenate(parts, axis=0)

        values, back = jax.vjp(
            lambda *table: project(list(table), camera),
            *[gauss_ref[k, here, :] for k in range(59)],
        )
        u, v, conic_a, conic_b, conic_c, opacity = values[:6]
        g_0, g_x, g_y, g_xx, g_xy, g_yy = [moment(k) for k in range(6)]
        u = u - moment(11)
        v = v - moment(12)
        s_x = g_x - u * g_0
        s_y = g_y - v * g_0
        s_xx = g_xx - u * (g_x + s_x)
        s_xy = g_xy - u * g_y - v * s_x
        s_yy = g_yy - v * (g_y + s_y)
        given = [
            conic_a * s_x + conic_b * s_y,
            conic_c * s_y + conic_b * s_x,
            -0.5 * s_xx,
            -s_xy,
            -0.5 * s_yy,
            g_0 / opacity,
        ] + [moment(8 + k) for k in range(3)]
        grads = back(given)
        for k in range(59):
            out_ref[k, here, :] = grads[k]


def exchange_kernel(sizes, in_ref, out_ref, send_sem, recv_sem, own_sem):
    n = sizes[0] * sizes[1]
    share = n // in_ref.shape[0]
    me = lax.axis_index("tile") * sizes[1] + lax.axis_index("shard")
    barrier = pltpu.get_barrier_semaphore()

    def greet(step, unused):
        peer = lax.rem(me + step, n)
        pl.semaphore_signal(
            barrier,
            inc=1,
            device_id=(peer // sizes[1], lax.rem(peer, sizes[1])),
            device_id_type=MESH,
        )
        return unused

    def transfer(step):
        peer = lax.rem(me + step, n)
        return pltpu.make_async_remote_copy(
            src_ref=in_ref.at[peer // share],
            dst_ref=out_ref.at[me],
            send_sem=send_sem.at[step],
            recv_sem=recv_sem.at[step],
            device_id=(peer // sizes[1], lax.rem(peer, sizes[1])),
            device_id_type=MESH,
        )

    def start(step, unused):
        transfer(step).start()
        return unused

    def finish(step, unused):
        transfer(step).wait()
        return unused

    own = pltpu.make_async_copy(in_ref.at[me // share], out_ref.at[me], own_sem)
    own.start()
    lax.fori_loop(1, n, greet, 0)
    pl.semaphore_wait(barrier, n - 1)
    lax.fori_loop(1, n, start, 0)
    lax.fori_loop(1, n, finish, 0)
    own.wait()


def exchange(blocks, sizes, number, name):
    n = sizes[0] * sizes[1]
    return pl.pallas_call(
        functools.partial(exchange_kernel, sizes),
        out_shape=jax.ShapeDtypeStruct((n,) + blocks.shape[1:], blocks.dtype),
        in_specs=[pl.BlockSpec(memory_space=pltpu.VMEM)],
        out_specs=pl.BlockSpec(memory_space=pltpu.VMEM),
        scratch_shapes=[
            pltpu.SemaphoreType.DMA((n,)),
            pltpu.SemaphoreType.DMA((n,)),
            pltpu.SemaphoreType.DMA,
        ],
        compiler_params=pltpu.CompilerParams(collective_id=number, has_side_effects=True),
        name=name,
    )(blocks)


def split(value):
    high = value.astype(jnp.bfloat16)
    return high, (value - high.astype(jnp.float32)).astype(jnp.bfloat16)


def times(left, right, dims):
    return lax.dot_general(left, right, dims, preferred_element_type=jnp.float32)


def render_kernel(
    ids_ref,
    counts_ref,
    active_ref,
    lists_ref,
    feat_ref,
    target_ref,
    pixel_ref,
    mono_ref,
    image_ref,
    out_ref,
    tab,
    rows,
    alphas,
    weights,
    powers,
    errors,
):
    need = feat_ref.shape[0] * HALF
    span = need // SEGMENTS
    slots = image_ref.shape[1]
    lane = lax.broadcasted_iota(jnp.int32, (1, 128), 1)

    for block in range(need // 128):
        lanes = slice(block * 128, block * 128 + 128)
        values = halves(feat_ref[2 * block], feat_ref[2 * block + 1])
        colours = [jnp.broadcast_to(values[6 + k : 7 + k, :], (16, 128)) for k in range(3)]
        tab[lanes, 0:WIDE] = jnp.concatenate([values] + colours, axis=0).T

    def centre(slot):
        tile = ids_ref[slot]
        centre_x = ((tile % TILES_X) * TILE_SIDE + TILE_SIDE // 2).astype(jnp.float32)
        centre_y = ((tile // TILES_X) * TILE_SIDE + TILE_SIDE // 2).astype(jnp.float32)
        return centre_x, centre_y

    def of_tile(slot):
        return (lane >= 16) & (lane < WIDE) & (lane % 16 == slot)

    bits = span.bit_length() - 1

    def places(slot, start, step):
        first = step * BATCH
        for part in range(BATCH):
            rank = first + part
            entry = start + rank
            row = ((entry & (span - 1)) << 4) | (entry >> bits)
            yield rank < counts_ref[slot], lists_ref[slot, rank], row

    def pick(slot, start):
        count = counts_ref[slot]
        centre_x, centre_y = centre(slot)
        alive = jnp.where(active_ref[slot] > 0, 1.0, 0.0)
        scale = jnp.where((lane < 5) | of_tile(slot), 1.0, jnp.where(lane == 5, alive, 0.0))
        offset = jnp.where(lane == 0, -centre_x, jnp.where(lane == 1, -centre_y, 0.0))
        offset = jnp.where(lane == 6, start.astype(jnp.float32), offset)
        offset = jnp.where(lane == 7, (start + count).astype(jnp.float32), offset)

        @pl.loop(0, (count + BATCH - 1) // BATCH)
        def _(step):
            found = list(places(slot, start, step))
            picked = [tab[pl.ds(place, 1), :] for used, place, row in found]
            for (used, place, row), value in zip(found, picked):
                rows[pl.ds(jnp.where(used, row, need), 1), :] = value * scale + offset

        return start + count

    lax.fori_loop(0, slots, pick, jnp.int32(0))

    pixel_x = jnp.broadcast_to(pixel_ref[0:1, :], (8, PIXELS))
    pixel_y = jnp.broadcast_to(pixel_ref[1:2, :], (8, PIXELS))
    sets = range(SEGMENTS // 8)
    sub = lax.broadcasted_iota(jnp.int32, (8, 1), 0)
    bases = [((sub + 8 * q) * span).astype(jnp.float32) for q in sets]
    one = jnp.ones((8, PIXELS), jnp.float32)
    zero = jnp.zeros((8, PIXELS), jnp.float32)

    def forward(step, state):
        left, seen = list(state[0]), list(state[1])
        for part in range(STEPS):
            place = step * STEPS + part
            for q in sets:
                here = pl.ds(pl.multiple_of(place * SEGMENTS + 8 * q, 8), 8)
                row = rows[here, :]
                delta_x = pixel_x - row[:, 0:1]
                delta_y = pixel_y - row[:, 1:2]
                power = (
                    delta_x * (row[:, 2:3] * delta_x + row[:, 3:4] * delta_y)
                    + row[:, 4:5] * delta_y * delta_y
                )
                alpha = row[:, 5:6] * jnp.exp(power)
                begins = jnp.where(row[:, 6:7] == bases[q] + place.astype(jnp.float32), 1.0, 0.0)
                seen[q] = jnp.maximum(seen[q], begins)
                passed = jnp.where(jnp.broadcast_to(begins, (8, PIXELS)) > 0.0, 1.0, left[q])
                alphas[here, :] = alpha
                weights[here, :] = alpha * passed
                left[q] = passed * (1.0 - alpha)
        return tuple(left), tuple(seen)

    none = jnp.zeros((8, 1), jnp.float32)
    left, seen = lax.fori_loop(
        0, span // STEPS, forward, (tuple(one for q in sets), tuple(none for q in sets))
    )
    carry = one[0:1, :]
    ahead = []
    for q in sets:
        parts = []
        for k in range(8):
            parts.append(carry)
            begun = seen[q][k : k + 1, :]
            carry = left[q][k : k + 1, :] * (begun + (1.0 - begun) * carry)
        ahead.append(jnp.concatenate(parts, axis=0))

    def composite(chunk, image):
        here = pl.ds(pl.multiple_of(chunk * CHUNK, CHUNK), CHUNK)
        for group in range(CHUNK // 8):
            q = group % len(sets)
            part = pl.ds(pl.multiple_of(chunk * CHUNK + 8 * group, 8), 8)
            head = jnp.where(rows[part, 6:7] < bases[q], 1.0, 0.0)
            factor = jnp.where(jnp.broadcast_to(head, (8, PIXELS)) > 0.0, ahead[q], 1.0)
            weights[part, :] = weights[part, :] * factor
        colour_high, colour_low = split(rows[here, 0:WIDE].T)
        weight_high, weight_low = split(weights[here, :])
        return (
            image
            + times(colour_low, weight_high, NN)
            + times(colour_high, weight_low, NN)
            + times(colour_high, weight_high, NN)
        )

    chunks = need // CHUNK
    image = lax.fori_loop(0, chunks, composite, jnp.zeros((WIDE, PIXELS), jnp.float32))
    errors[0:16, :] = jnp.zeros((16, PIXELS), jnp.float32)
    for k in range(3):
        part = image[16 + 16 * k : 32 + 16 * k, :]
        image_ref[k] = part
        errors[16 + 16 * k : 32 + 16 * k, :] = part - target_ref[k]

    def backward(step, later):
        later = list(later)
        chunk = chunks - 1 - step
        here = pl.ds(pl.multiple_of(chunk * CHUNK, CHUNK), CHUNK)
        colour_high, colour_low = split(rows[here, 0:WIDE])
        error_high, error_low = split(errors[...])
        powers[here, :] = (
            times(colour_low, error_high, NN)
            + times(colour_high, error_low, NN)
            + times(colour_high, error_high, NN)
        )
        for group in reversed(range(CHUNK // 8)):
            q = group % len(sets)
            part = pl.ds(pl.multiple_of(chunk * CHUNK + 8 * group, 8), 8)
            after = (chunk * (CHUNK // SEGMENTS) + group // len(sets) + 1).astype(jnp.float32)
            ends = jnp.where(rows[part, 7:8] == bases[q] + after, 1.0, 0.0)
            alpha = alphas[part, :]
            given = weights[part, :] * powers[part, :]
            rest = jnp.where(jnp.broadcast_to(ends, (8, PIXELS)) > 0.0, 0.0, later[q])
            ratio = alpha / (1.0 - alpha)
            alphas[part, :] = ratio
            powers[part, :] = given - ratio * rest
            later[q] = rest + given
        return tuple(later)

    later = lax.fori_loop(0, chunks, backward, tuple(zero for q in sets))
    carry = zero[0:1, :]
    behind = []
    for q in reversed(sets):
        final = pl.ds((span - 1) * SEGMENTS + 8 * q, 8)
        onward = jnp.where(rows[final, 7:8] > bases[q] + span, 1.0, 0.0) * (1.0 - seen[q])
        parts = []
        for k in reversed(range(8)):
            parts.append(carry)
            carry = later[q][k : k + 1, :] + onward[k : k + 1, :] * carry
        behind.append(jnp.concatenate(parts[::-1], axis=0))
    behind = behind[::-1]

    @pl.loop(0, chunks)
    def _(chunk):
        here = pl.ds(pl.multiple_of(chunk * CHUNK, CHUNK), CHUNK)
        for group in range(CHUNK // 8):
            q = group % len(sets)
            part = pl.ds(pl.multiple_of(chunk * CHUNK + 8 * group, 8), 8)
            tail = jnp.where(rows[part, 7:8] > bases[q] + span, 1.0, 0.0)
            rest = jnp.where(jnp.broadcast_to(tail, (8, PIXELS)) > 0.0, behind[q], 0.0)
            powers[part, :] = powers[part, :] - alphas[part, :] * rest
        power_high, power_low = split(powers[here, :])
        weight_high, weight_low = split(weights[here, :])
        error_high, error_low = split(errors[...])
        mono = mono_ref[...].astype(jnp.bfloat16)
        rows[here, 0:WIDE] = (
            times(power_low, mono, NT)
            + times(weight_low, error_high, NT)
            + times(weight_high, error_low, NT)
            + times(power_high, mono, NT)
            + times(weight_high, error_high, NT)
        )

    def put(slot, start):
        count = counts_ref[slot]
        centre_x, centre_y = centre(slot)
        scale = jnp.where((lane < 6) | of_tile(slot), 1.0, 0.0)
        offset = jnp.where(lane == 11, centre_x, jnp.where(lane == 12, centre_y, 0.0))

        @pl.loop(0, (count + BATCH - 1) // BATCH)
        def _(step):
            found = list(places(slot, start, step))
            picked = [rows[pl.ds(row, 1), :] for used, place, row in found]
            for (used, place, row), value in zip(found, picked):
                tab[pl.ds(jnp.where(used, place, need), 1), :] = value * scale + offset

        return start + count

    lax.fori_loop(0, slots, put, jnp.int32(0))
    sub = lax.broadcasted_iota(jnp.int32, (8, 128), 0)
    for block in range(need // 128):
        lanes = slice(block * 128, block * 128 + 128)
        values = tab[lanes, 0:WIDE].T
        low = values[8:16, :]
        for k in range(3):
            summed = jnp.sum(values[16 + 16 * k : 32 + 16 * k, :], axis=0, keepdims=True)
            low = jnp.where(sub == k, summed, low)
        first, second = packed(jnp.concatenate([values[0:8, :], low], axis=0))
        out_ref[2 * block] = first
        out_ref[2 * block + 1] = second


def render(features, tiles, lists, counts, active, target):
    need = features.shape[0] * HALF
    if target.shape[1] != 16 or need % (SEGMENTS * 128) != 0:
        raise ValueError("unsupported sizes")
    spot = np.arange(PIXELS)
    local_x = spot % TILE_SIDE + 0.5 - TILE_SIDE // 2
    local_y = spot // TILE_SIDE + 0.5 - TILE_SIDE // 2
    pixel = np.zeros((8, PIXELS), np.float32)
    pixel[0], pixel[1] = local_x, local_y
    mono = np.zeros((WIDE, PIXELS), np.float32)
    mono[0] = 1.0
    mono[1], mono[2] = local_x, local_y
    mono[3], mono[4], mono[5] = local_x * local_x, local_x * local_y, local_y * local_y
    smem = pl.BlockSpec(memory_space=pltpu.SMEM)
    vmem = pl.BlockSpec(memory_space=pltpu.VMEM)
    return pl.pallas_call(
        render_kernel,
        out_shape=(
            jax.ShapeDtypeStruct(target.shape, jnp.float32),
            jax.ShapeDtypeStruct(features.shape, jnp.float32),
        ),
        in_specs=[smem] * 4 + [vmem] * 4,
        out_specs=(vmem, vmem),
        scratch_shapes=[
            pltpu.VMEM((need + 8, 128), jnp.float32),
            pltpu.VMEM((need + 8, 128), jnp.float32),
            pltpu.VMEM((need, PIXELS), jnp.float32),
            pltpu.VMEM((need, PIXELS), jnp.float32),
            pltpu.VMEM((need, PIXELS), jnp.float32),
            pltpu.VMEM((WIDE, PIXELS), jnp.float32),
        ],
        compiler_params=pltpu.CompilerParams(vmem_limit_bytes=48 * 1024 * 1024),
        name="render",
    )(tiles, counts, active, lists, features, target, jnp.asarray(pixel), jnp.asarray(mono))


def per_device(
    sizes,
    gaussians,
    camera,
    fetch_index,
    tile_ids,
    tile_lists,
    tile_counts,
    tile_active,
    target,
):
    owned = gaussians.shape[1]
    need = fetch_index.shape[1]
    n = sizes[0] * sizes[1]
    if need != n * HALF or owned % 1024 != 0:
        raise ValueError("unsupported sizes")
    smem = pl.BlockSpec(memory_space=pltpu.SMEM)
    vmem = pl.BlockSpec(memory_space=pltpu.VMEM)
    slabs = gaussians.reshape(59, owned // 128, 128)
    params = pltpu.CompilerParams(vmem_limit_bytes=40 * 1024 * 1024)
    me = lax.axis_index("tile") * sizes[1] + lax.axis_index("shard")
    shift = (lax.rem(me, 2) * HALF).astype(jnp.int32).reshape(1)
    asked = exchange(fetch_index.reshape(n // 2, 1, 128), sizes, 0, "ask").reshape(n, 128)
    offered = pl.pallas_call(
        offer_kernel,
        out_shape=jax.ShapeDtypeStruct((n, 8, 128), jnp.float32),
        in_specs=[smem, smem, smem, vmem],
        out_specs=vmem,
        scratch_shapes=[
            pltpu.VMEM((PACK, owned), jnp.float32),
            pltpu.VMEM((owned, 128), jnp.float32),
            pltpu.VMEM((128, 128), jnp.float32),
        ],
        compiler_params=params,
        name="offer",
    )(camera, asked, shift, slabs)
    table = exchange(offered, sizes, 1, "fetch")
    image, moments = render(
        table, tile_ids[0], tile_lists[0], tile_counts[0], tile_active[0], target
    )
    returned = exchange(moments, sizes, 2, "give")
    grads = pl.pallas_call(
        settle_kernel,
        out_shape=jax.ShapeDtypeStruct(slabs.shape, jnp.float32),
        in_specs=[smem, smem, smem, vmem, vmem],
        out_specs=vmem,
        scratch_shapes=[
            pltpu.VMEM((owned, 128), jnp.float32),
            pltpu.VMEM((128, 128), jnp.float32),
            pltpu.VMEM((PACK, owned), jnp.float32),
        ],
        compiler_params=params,
        name="settle",
    )(camera, asked, shift, slabs, returned)
    return (image, grads.reshape(gaussians.shape))


def solution(mesh):
    in_specs = (
        P(None, ("tile", "shard")),
        P(),
        P(("tile", "shard"), None),
        P(("tile", "shard"), None),
        P(("tile", "shard"), None, None),
        P(("tile", "shard"), None),
        P(("tile", "shard"), None),
        P(None, ("tile", "shard"), None),
    )
    out_specs = (P(None, ("tile", "shard"), None), P(None, ("tile", "shard")))
    sizes = (mesh.shape["tile"], mesh.shape["shard"])
    return jax.shard_map(
        functools.partial(per_device, sizes), mesh=mesh, in_specs=in_specs, out_specs=out_specs, check_vma=False
    )
```

```python
import functools

import jax
import jax.numpy as jnp
import numpy as np
from jax import lax
from jax.experimental import pallas as pl
from jax.experimental.pallas import tpu as pltpu
from jax.sharding import PartitionSpec as P

TILE_SIDE = 16
TILES_X = 64
PIXELS = TILE_SIDE * TILE_SIDE
PACK = 16
HALF = 64
WIDE = 64
SEGMENTS = 16
STEPS = 8
BATCH = 16
CHUNK = 256
NN = (((1,), (0,)), ((), ()))
NT = (((1,), (1,)), ((), ()))
MESH = pl.DeviceIdType.MESH


SH_ZERO = 0.28209479177387814
SH_ONE = 0.4886025119029199
SH_TWO = (
    1.0925484305920792,
    -1.0925484305920792,
    0.31539156525252005,
    -1.0925484305920792,
    0.5462742152960396,
)
SH_THREE = (
    -0.5900435899266435,
    2.890611442640554,
    -0.4570457994644658,
    0.3731763325901154,
    -0.4570457994644658,
    1.445305721320277,
    -0.5900435899266435,
)


def harmonics(dir_x, dir_y, dir_z):
    sq_x, sq_y, sq_z = (dir_x * dir_x, dir_y * dir_y, dir_z * dir_z)
    rows = [
        SH_ZERO * jnp.ones_like(dir_x),
        -SH_ONE * dir_y,
        SH_ONE * dir_z,
        -SH_ONE * dir_x,
        SH_TWO[0] * dir_x * dir_y,
        SH_TWO[1] * dir_y * dir_z,
        SH_TWO[2] * (2.0 * sq_z - sq_x - sq_y),
        SH_TWO[3] * dir_x * dir_z,
        SH_TWO[4] * (sq_x - sq_y),
        SH_THREE[0] * dir_y * (3.0 * sq_x - sq_y),
        SH_THREE[1] * dir_x * dir_y * dir_z,
        SH_THREE[2] * dir_y * (4.0 * sq_z - sq_x - sq_y),
        SH_THREE[3] * dir_z * (2.0 * sq_z - 3.0 * sq_x - 3.0 * sq_y),
        SH_THREE[4] * dir_x * (4.0 * sq_z - sq_x - sq_y),
        SH_THREE[5] * dir_z * (sq_x - sq_y),
        SH_THREE[6] * dir_x * (sq_x - 3.0 * sq_y),
    ]
    return rows


def project(table, camera):
    focal_x, focal_y, centre_x, centre_y = camera
    mean_x, mean_y, mean_z = table[0:3]
    spread = [jnp.exp(value) for value in table[3:6]]
    quat = table[6:10]
    length = jnp.sqrt(
        quat[0] * quat[0] + quat[1] * quat[1] + quat[2] * quat[2] + quat[3] * quat[3]
    )
    inverse = 1.0 / length
    w_part, x_part, y_part, z_part = [value * inverse for value in quat]
    rotate = [
        [
            1.0 - 2.0 * (y_part * y_part + z_part * z_part),
            2.0 * (x_part * y_part - w_part * z_part),
            2.0 * (x_part * z_part + w_part * y_part),
        ],
        [
            2.0 * (x_part * y_part + w_part * z_part),
            1.0 - 2.0 * (x_part * x_part + z_part * z_part),
            2.0 * (y_part * z_part - w_part * x_part),
        ],
        [
            2.0 * (x_part * z_part - w_part * y_part),
            2.0 * (y_part * z_part + w_part * x_part),
            1.0 - 2.0 * (x_part * x_part + y_part * y_part),
        ],
    ]
    scaled = [[rotate[row][col] * spread[col] for col in range(3)] for row in range(3)]
    depth_inv = 1.0 / mean_z
    ratio_x = mean_x * depth_inv
    ratio_y = mean_y * depth_inv
    scale_x = focal_x * depth_inv
    scale_y = focal_y * depth_inv
    top = [scale_x * (scaled[0][col] - ratio_x * scaled[2][col]) for col in range(3)]
    low = [scale_y * (scaled[1][col] - ratio_y * scaled[2][col]) for col in range(3)]
    cov_a = top[0] * top[0] + top[1] * top[1] + top[2] * top[2] + 0.3
    cov_b = top[0] * low[0] + top[1] * low[1] + top[2] * low[2]
    cov_c = low[0] * low[0] + low[1] * low[1] + low[2] * low[2] + 0.3
    det_inv = 1.0 / (cov_a * cov_c - cov_b * cov_b)
    screen_x = focal_x * ratio_x + centre_x
    screen_y = focal_y * ratio_y + centre_y
    opacity = 1.0 / (1.0 + jnp.exp(-table[10]))
    radius_inv = 1.0 / jnp.sqrt(mean_x * mean_x + mean_y * mean_y + mean_z * mean_z)
    basis = harmonics(mean_x * radius_inv, mean_y * radius_inv, mean_z * radius_inv)
    colours = []
    for channel in range(3):
        total = table[11 + 16 * channel] * basis[0]
        for term in range(1, 16):
            total = total + table[11 + 16 * channel + term] * basis[term]
        colours.append(jnp.maximum(total + 0.5, 0.0))
    return [
        screen_x,
        screen_y,
        cov_c * det_inv,
        -cov_b * det_inv,
        cov_a * det_inv,
        opacity,
    ] + colours


def halves(first, second):
    lane = lax.broadcasted_iota(jnp.int32, (8, 128), 1)
    top = jnp.where(lane < HALF, first, pltpu.roll(second, HALF, 1))
    low = jnp.where(lane < HALF, pltpu.roll(first, HALF, 1), second)
    return jnp.concatenate([top, low], axis=0)


def packed(block):
    lane = lax.broadcasted_iota(jnp.int32, (8, 128), 1)
    top, low = block[0:8, :], block[8:16, :]
    first = jnp.where(lane < HALF, top, pltpu.roll(low, HALF, 1))
    second = jnp.where(lane < HALF, pltpu.roll(top, HALF, 1), low)
    return first, second


def offer_kernel(camera_ref, asked_ref, shift_ref, gauss_ref, out_ref, feat, tab, rows):
    camera = [camera_ref[k] for k in range(4)]
    shift = shift_ref[0]
    feat[...] = jnp.zeros_like(feat)

    @pl.loop(0, gauss_ref.shape[1] // 8)
    def _(slab):
        here = pl.ds(pl.multiple_of(slab * 8, 8), 8)
        values = project([gauss_ref[k, here, :] for k in range(59)], camera)
        u, v, conic_a, conic_b, conic_c, opacity = values[:6]
        sent = [u, v, -0.5 * conic_a, -conic_b, -0.5 * conic_c, opacity] + values[6:]
        for r in range(8):
            lanes = pl.ds(pl.multiple_of(slab * 1024 + r * 128, 128), 128)
            for k in range(9):
                feat[k : k + 1, lanes] = sent[k][r : r + 1, :]

    for block in range(tab.shape[0] // 128):
        lanes = slice(block * 128, block * 128 + 128)
        tab[lanes, 0:PACK] = feat[:, lanes].T

    @pl.loop(0, out_ref.shape[0] // 2)
    def _(pair):
        for half in range(2):
            for k in range(0, HALF, BATCH):
                picked = [
                    tab[pl.ds(asked_ref[2 * pair + half, shift + k + part], 1), :]
                    for part in range(BATCH)
                ]
                first = half * HALF + k
                rows[first : first + BATCH, :] = jnp.concatenate(picked, axis=0)
        first, second = packed(rows[:, 0:PACK].T)
        out_ref[2 * pair] = first
        out_ref[2 * pair + 1] = second


def settle_kernel(camera_ref, asked_ref, shift_ref, gauss_ref, moment_ref, out_ref, tab, rows, sums):
    camera = [camera_ref[k] for k in range(4)]
    shift = shift_ref[0]

    @pl.loop(0, moment_ref.shape[0] // 2)
    def _(pair):
        rows[:, 0:PACK] = halves(moment_ref[2 * pair], moment_ref[2 * pair + 1]).T
        for half in range(2):
            for k in range(0, HALF, BATCH):
                first = half * HALF + k
                block = rows[first : first + BATCH, :]
                for part in range(BATCH):
                    place = asked_ref[2 * pair + half, shift + k + part]
                    tab[pl.ds(place, 1), :] = block[part : part + 1, :]

    for block in range(tab.shape[0] // 128):
        lanes = slice(block * 128, block * 128 + 128)
        sums[:, lanes] = tab[lanes, 0:PACK].T

    @pl.loop(0, gauss_ref.shape[1] // 8)
    def _(slab):
        here = pl.ds(pl.multiple_of(slab * 8, 8), 8)

        def moment(k):
            parts = [
                sums[k : k + 1, pl.ds(pl.multiple_of(slab * 1024 + r * 128, 128), 128)]
                for r in range(8)
            ]
            return jnp.concatenate(parts, axis=0)

        values, back = jax.vjp(
            lambda *table: project(list(table), camera),
            *[gauss_ref[k, here, :] for k in range(59)],
        )
        u, v, conic_a, conic_b, conic_c, opacity = values[:6]
        g_0, g_x, g_y, g_xx, g_xy, g_yy = [moment(k) for k in range(6)]
        u = u - moment(11)
        v = v - moment(12)
        s_x = g_x - u * g_0
        s_y = g_y - v * g_0
        s_xx = g_xx - u * (g_x + s_x)
        s_xy = g_xy - u * g_y - v * s_x
        s_yy = g_yy - v * (g_y + s_y)
        given = [
            conic_a * s_x + conic_b * s_y,
            conic_c * s_y + conic_b * s_x,
            -0.5 * s_xx,
            -s_xy,
            -0.5 * s_yy,
            g_0 / opacity,
        ] + [moment(8 + k) for k in range(3)]
        grads = back(given)
        for k in range(59):
            out_ref[k, here, :] = grads[k]


def exchange_kernel(sizes, in_ref, out_ref, send_sem, recv_sem, own_sem):
    n = sizes[0] * sizes[1]
    share = (n // in_ref.shape[0]).bit_length() - 1
    bits = sizes[1].bit_length() - 1
    me = (lax.axis_index("tile") << bits) | lax.axis_index("shard")
    barrier = pltpu.get_barrier_semaphore()

    def place(peer):
        return (peer >> bits, peer & (sizes[1] - 1))

    def greet(step, unused):
        peer = (me + step) & (n - 1)
        pl.semaphore_signal(barrier, inc=1, device_id=place(peer), device_id_type=MESH)
        return unused

    def start(step, unused):
        peer = (me + step) & (n - 1)
        pltpu.make_async_remote_copy(
            src_ref=in_ref.at[peer >> share],
            dst_ref=out_ref.at[me],
            send_sem=send_sem,
            recv_sem=recv_sem,
            device_id=place(peer),
            device_id_type=MESH,
        ).start()
        return unused

    own = pltpu.make_async_copy(in_ref.at[me >> share], out_ref.at[me], own_sem)
    own.start()
    lax.fori_loop(1, n, greet, 0)
    pl.semaphore_wait(barrier, n - 1)
    lax.fori_loop(1, n, start, 0)
    own.wait()
    others = out_ref.at[pl.ds(0, n - 1)]
    pltpu.make_async_copy(others, others, send_sem).wait()
    pltpu.make_async_copy(others, others, recv_sem).wait()


def exchange(blocks, sizes, number, name):
    n = sizes[0] * sizes[1]
    return pl.pallas_call(
        functools.partial(exchange_kernel, sizes),
        out_shape=jax.ShapeDtypeStruct((n,) + blocks.shape[1:], blocks.dtype),
        in_specs=[pl.BlockSpec(memory_space=pltpu.VMEM)],
        out_specs=pl.BlockSpec(memory_space=pltpu.VMEM),
        scratch_shapes=[
            pltpu.SemaphoreType.DMA,
            pltpu.SemaphoreType.DMA,
            pltpu.SemaphoreType.DMA,
        ],
        compiler_params=pltpu.CompilerParams(collective_id=number, has_side_effects=True),
        name=name,
    )(blocks)


def split(value):
    high = value.astype(jnp.bfloat16)
    return high, (value - high.astype(jnp.float32)).astype(jnp.bfloat16)


def times(left, right, dims):
    return lax.dot_general(left, right, dims, preferred_element_type=jnp.float32)


def render_kernel(
    ids_ref,
    counts_ref,
    active_ref,
    lists_ref,
    feat_ref,
    target_ref,
    pixel_ref,
    mono_ref,
    image_ref,
    out_ref,
    tab,
    line,
    rows,
    alphas,
    weights,
    powers,
    errors,
):
    need = feat_ref.shape[0] * HALF
    span = need // SEGMENTS
    slots = image_ref.shape[1]
    lane = lax.broadcasted_iota(jnp.int32, (1, 128), 1)

    for block in range(need // 128):
        lanes = slice(block * 128, block * 128 + 128)
        values = halves(feat_ref[2 * block], feat_ref[2 * block + 1])
        colours = [jnp.broadcast_to(values[6 + k : 7 + k, :], (16, 128)) for k in range(3)]
        tab[lanes, 0:WIDE] = jnp.concatenate([values] + colours, axis=0).T

    def centre(slot):
        tile = ids_ref[slot]
        centre_x = ((tile % TILES_X) * TILE_SIDE + TILE_SIDE // 2).astype(jnp.float32)
        centre_y = ((tile // TILES_X) * TILE_SIDE + TILE_SIDE // 2).astype(jnp.float32)
        return centre_x, centre_y

    def of_tile(slot):
        return (lane >= 16) & (lane < WIDE) & (lane % 16 == slot)

    def pick(slot, start):
        count = counts_ref[slot]
        centre_x, centre_y = centre(slot)
        alive = jnp.where(active_ref[slot] > 0, 1.0, 0.0)
        scale = jnp.where((lane < 5) | of_tile(slot), 1.0, jnp.where(lane == 5, alive, 0.0))
        offset = jnp.where(lane == 0, -centre_x, jnp.where(lane == 1, -centre_y, 0.0))
        offset = jnp.where(lane == 6, start.astype(jnp.float32), offset)
        offset = jnp.where(lane == 7, (start + count).astype(jnp.float32), offset)

        @pl.loop(0, (count + BATCH - 1) // BATCH)
        def _(step):
            first = step * BATCH
            picked = [
                tab[pl.ds(lists_ref[slot, first + part], 1), :] for part in range(BATCH)
            ]
            block = jnp.concatenate(picked, axis=0) * scale + offset
            line[pl.ds(start + first, BATCH), :] = block

        return start + count

    lax.fori_loop(0, slots, pick, jnp.int32(0))
    for segment in range(SEGMENTS):
        whole = slice(segment * span, segment * span + span)
        rows[pl.ds(segment, span, stride=SEGMENTS), :] = line[whole, :]

    pixel_x = jnp.broadcast_to(pixel_ref[0:1, :], (8, PIXELS))
    pixel_y = jnp.broadcast_to(pixel_ref[1:2, :], (8, PIXELS))
    sets = range(SEGMENTS // 8)
    sub = lax.broadcasted_iota(jnp.int32, (8, 1), 0)
    bases = [((sub + 8 * q) * span).astype(jnp.float32) for q in sets]
    one = jnp.ones((8, PIXELS), jnp.float32)
    zero = jnp.zeros((8, PIXELS), jnp.float32)

    def forward(step, state):
        left, seen = list(state[0]), list(state[1])
        for part in range(STEPS):
            place = step * STEPS + part
            for q in sets:
                here = pl.ds(pl.multiple_of(place * SEGMENTS + 8 * q, 8), 8)
                row = rows[here, :]
                delta_x = pixel_x - row[:, 0:1]
                delta_y = pixel_y - row[:, 1:2]
                power = (
                    delta_x * (row[:, 2:3] * delta_x + row[:, 3:4] * delta_y)
                    + row[:, 4:5] * delta_y * delta_y
                )
                alpha = row[:, 5:6] * jnp.exp(power)
                begins = jnp.where(row[:, 6:7] == bases[q] + place.astype(jnp.float32), 1.0, 0.0)
                seen[q] = jnp.maximum(seen[q], begins)
                passed = jnp.where(jnp.broadcast_to(begins, (8, PIXELS)) > 0.0, 1.0, left[q])
                alphas[here, :] = alpha
                weights[here, :] = alpha * passed
                left[q] = passed * (1.0 - alpha)
        return tuple(left), tuple(seen)

    none = jnp.zeros((8, 1), jnp.float32)
    left, seen = lax.fori_loop(
        0, span // STEPS, forward, (tuple(one for q in sets), tuple(none for q in sets))
    )
    carry = one[0:1, :]
    ahead = []
    for q in sets:
        parts = []
        for k in range(8):
            parts.append(carry)
            begun = seen[q][k : k + 1, :]
            carry = left[q][k : k + 1, :] * (begun + (1.0 - begun) * carry)
        ahead.append(jnp.concatenate(parts, axis=0))

    def composite(chunk, image):
        here = pl.ds(pl.multiple_of(chunk * CHUNK, CHUNK), CHUNK)
        for group in range(CHUNK // 8):
            q = group % len(sets)
            part = pl.ds(pl.multiple_of(chunk * CHUNK + 8 * group, 8), 8)
            head = jnp.where(rows[part, 6:7] < bases[q], 1.0, 0.0)
            factor = jnp.where(jnp.broadcast_to(head, (8, PIXELS)) > 0.0, ahead[q], 1.0)
            weights[part, :] = weights[part, :] * factor
        colour_high, colour_low = split(rows[here, 0:WIDE].T)
        weight_high, weight_low = split(weights[here, :])
        return (
            image
            + times(colour_low, weight_high, NN)
            + times(colour_high, weight_low, NN)
            + times(colour_high, weight_high, NN)
        )

    chunks = need // CHUNK
    image = lax.fori_loop(0, chunks, composite, jnp.zeros((WIDE, PIXELS), jnp.float32))
    errors[0:16, :] = jnp.zeros((16, PIXELS), jnp.float32)
    for k in range(3):
        part = image[16 + 16 * k : 32 + 16 * k, :]
        image_ref[k] = part
        errors[16 + 16 * k : 32 + 16 * k, :] = part - target_ref[k]

    def backward(step, later):
        later = list(later)
        chunk = chunks - 1 - step
        here = pl.ds(pl.multiple_of(chunk * CHUNK, CHUNK), CHUNK)
        colour_high, colour_low = split(rows[here, 0:WIDE])
        error_high, error_low = split(errors[...])
        powers[here, :] = (
            times(colour_low, error_high, NN)
            + times(colour_high, error_low, NN)
            + times(colour_high, error_high, NN)
        )
        for group in reversed(range(CHUNK // 8)):
            q = group % len(sets)
            part = pl.ds(pl.multiple_of(chunk * CHUNK + 8 * group, 8), 8)
            after = (chunk * (CHUNK // SEGMENTS) + group // len(sets) + 1).astype(jnp.float32)
            ends = jnp.where(rows[part, 7:8] == bases[q] + after, 1.0, 0.0)
            alpha = alphas[part, :]
            given = weights[part, :] * powers[part, :]
            rest = jnp.where(jnp.broadcast_to(ends, (8, PIXELS)) > 0.0, 0.0, later[q])
            ratio = alpha / (1.0 - alpha)
            alphas[part, :] = ratio
            powers[part, :] = given - ratio * rest
            later[q] = rest + given
        return tuple(later)

    later = lax.fori_loop(0, chunks, backward, tuple(zero for q in sets))
    carry = zero[0:1, :]
    behind = []
    for q in reversed(sets):
        final = pl.ds((span - 1) * SEGMENTS + 8 * q, 8)
        onward = jnp.where(rows[final, 7:8] > bases[q] + span, 1.0, 0.0) * (1.0 - seen[q])
        parts = []
        for k in reversed(range(8)):
            parts.append(carry)
            carry = later[q][k : k + 1, :] + onward[k : k + 1, :] * carry
        behind.append(jnp.concatenate(parts[::-1], axis=0))
    behind = behind[::-1]

    @pl.loop(0, chunks)
    def _(chunk):
        here = pl.ds(pl.multiple_of(chunk * CHUNK, CHUNK), CHUNK)
        for group in range(CHUNK // 8):
            q = group % len(sets)
            part = pl.ds(pl.multiple_of(chunk * CHUNK + 8 * group, 8), 8)
            tail = jnp.where(rows[part, 7:8] > bases[q] + span, 1.0, 0.0)
            rest = jnp.where(jnp.broadcast_to(tail, (8, PIXELS)) > 0.0, behind[q], 0.0)
            powers[part, :] = powers[part, :] - alphas[part, :] * rest
        power_high, power_low = split(powers[here, :])
        weight_high, weight_low = split(weights[here, :])
        error_high, error_low = split(errors[...])
        mono = mono_ref[...].astype(jnp.bfloat16)
        rows[here, 0:WIDE] = (
            times(power_low, mono, NT)
            + times(weight_low, error_high, NT)
            + times(weight_high, error_low, NT)
            + times(power_high, mono, NT)
            + times(weight_high, error_high, NT)
        )

    for segment in range(SEGMENTS):
        whole = slice(segment * span, segment * span + span)
        line[whole, :] = rows[pl.ds(segment, span, stride=SEGMENTS), :]

    def put(slot, start):
        count = counts_ref[slot]
        centre_x, centre_y = centre(slot)
        scale = jnp.where((lane < 6) | of_tile(slot), 1.0, 0.0)
        offset = jnp.where(lane == 11, centre_x, jnp.where(lane == 12, centre_y, 0.0))

        @pl.loop(0, (count + BATCH - 1) // BATCH)
        def _(step):
            first = step * BATCH
            block = line[pl.ds(start + first, BATCH), :] * scale + offset
            for part in range(BATCH):
                place = lists_ref[slot, first + part]
                place = jnp.where(first + part < count, place, need)
                tab[pl.ds(place, 1), :] = block[part : part + 1, :]

        return start + count

    lax.fori_loop(0, slots, put, jnp.int32(0))
    sub = lax.broadcasted_iota(jnp.int32, (8, 128), 0)
    for block in range(need // 128):
        lanes = slice(block * 128, block * 128 + 128)
        values = tab[lanes, 0:WIDE].T
        low = values[8:16, :]
        for k in range(3):
            summed = jnp.sum(values[16 + 16 * k : 32 + 16 * k, :], axis=0, keepdims=True)
            low = jnp.where(sub == k, summed, low)
        first, second = packed(jnp.concatenate([values[0:8, :], low], axis=0))
        out_ref[2 * block] = first
        out_ref[2 * block + 1] = second


def render(features, tiles, lists, counts, active, target):
    need = features.shape[0] * HALF
    if target.shape[1] != 16 or need % (SEGMENTS * 128) != 0:
        raise ValueError("unsupported sizes")
    spot = np.arange(PIXELS)
    local_x = spot % TILE_SIDE + 0.5 - TILE_SIDE // 2
    local_y = spot // TILE_SIDE + 0.5 - TILE_SIDE // 2
    pixel = np.zeros((8, PIXELS), np.float32)
    pixel[0], pixel[1] = local_x, local_y
    mono = np.zeros((WIDE, PIXELS), np.float32)
    mono[0] = 1.0
    mono[1], mono[2] = local_x, local_y
    mono[3], mono[4], mono[5] = local_x * local_x, local_x * local_y, local_y * local_y
    smem = pl.BlockSpec(memory_space=pltpu.SMEM)
    vmem = pl.BlockSpec(memory_space=pltpu.VMEM)
    return pl.pallas_call(
        render_kernel,
        out_shape=(
            jax.ShapeDtypeStruct(target.shape, jnp.float32),
            jax.ShapeDtypeStruct(features.shape, jnp.float32),
        ),
        in_specs=[smem] * 4 + [vmem] * 4,
        out_specs=(vmem, vmem),
        scratch_shapes=[
            pltpu.VMEM((need + 8, 128), jnp.float32),
            pltpu.VMEM((need + BATCH, 128), jnp.float32),
            pltpu.VMEM((need, 128), jnp.float32),
            pltpu.VMEM((need, PIXELS), jnp.float32),
            pltpu.VMEM((need, PIXELS), jnp.float32),
            pltpu.VMEM((need, PIXELS), jnp.float32),
            pltpu.VMEM((WIDE, PIXELS), jnp.float32),
        ],
        compiler_params=pltpu.CompilerParams(vmem_limit_bytes=48 * 1024 * 1024),
        name="render",
    )(tiles, counts, active, lists, features, target, jnp.asarray(pixel), jnp.asarray(mono))


def per_device(
    sizes,
    gaussians,
    camera,
    fetch_index,
    tile_ids,
    tile_lists,
    tile_counts,
    tile_active,
    target,
):
    owned = gaussians.shape[1]
    need = fetch_index.shape[1]
    n = sizes[0] * sizes[1]
    if sizes[1] & (sizes[1] - 1) or n & (n - 1):
        raise ValueError("unsupported mesh")
    if need != n * HALF or owned % 1024 != 0:
        raise ValueError("unsupported sizes")
    smem = pl.BlockSpec(memory_space=pltpu.SMEM)
    vmem = pl.BlockSpec(memory_space=pltpu.VMEM)
    slabs = gaussians.reshape(59, owned // 128, 128)
    params = pltpu.CompilerParams(vmem_limit_bytes=40 * 1024 * 1024)
    me = lax.axis_index("tile") * sizes[1] + lax.axis_index("shard")
    shift = (lax.rem(me, 2) * HALF).astype(jnp.int32).reshape(1)
    asked = exchange(fetch_index.reshape(n // 2, 1, 128), sizes, 0, "ask").reshape(n, 128)
    offered = pl.pallas_call(
        offer_kernel,
        out_shape=jax.ShapeDtypeStruct((n, 8, 128), jnp.float32),
        in_specs=[smem, smem, smem, vmem],
        out_specs=vmem,
        scratch_shapes=[
            pltpu.VMEM((PACK, owned), jnp.float32),
            pltpu.VMEM((owned, 128), jnp.float32),
            pltpu.VMEM((128, 128), jnp.float32),
        ],
        compiler_params=params,
        name="offer",
    )(camera, asked, shift, slabs)
    table = exchange(offered, sizes, 1, "fetch")
    image, moments = render(
        table, tile_ids[0], tile_lists[0], tile_counts[0], tile_active[0], target
    )
    returned = exchange(moments, sizes, 2, "give")
    grads = pl.pallas_call(
        settle_kernel,
        out_shape=jax.ShapeDtypeStruct(slabs.shape, jnp.float32),
        in_specs=[smem, smem, smem, vmem, vmem],
        out_specs=vmem,
        scratch_shapes=[
            pltpu.VMEM((owned, 128), jnp.float32),
            pltpu.VMEM((128, 128), jnp.float32),
            pltpu.VMEM((PACK, owned), jnp.float32),
        ],
        compiler_params=params,
        name="settle",
    )(camera, asked, shift, slabs, returned)
    return (image, grads.reshape(gaussians.shape))


def solution(mesh):
    in_specs = (
        P(None, ("tile", "shard")),
        P(),
        P(("tile", "shard"), None),
        P(("tile", "shard"), None),
        P(("tile", "shard"), None, None),
        P(("tile", "shard"), None),
        P(("tile", "shard"), None),
        P(None, ("tile", "shard"), None),
    )
    out_specs = (P(None, ("tile", "shard"), None), P(None, ("tile", "shard")))
    sizes = (mesh.shape["tile"], mesh.shape["shard"])
    return jax.shard_map(
        functools.partial(per_device, sizes), mesh=mesh, in_specs=in_specs, out_specs=out_specs, check_vma=False
    )
```

```python
import functools

import jax
import jax.numpy as jnp
import numpy as np
from jax import lax
from jax.experimental import pallas as pl
from jax.experimental.pallas import tpu as pltpu
from jax.sharding import PartitionSpec as P

TILE_SIDE = 16
TILES_X = 64
PIXELS = TILE_SIDE * TILE_SIDE
PACK = 16
HALF = 64
WIDE = 64
SEGMENTS = 16
STEPS = 8
BATCH = 16
CHUNK = 256
NN = (((1,), (0,)), ((), ()))
NT = (((1,), (1,)), ((), ()))
MESH = pl.DeviceIdType.MESH


SH_ZERO = 0.28209479177387814
SH_ONE = 0.4886025119029199
SH_TWO = (
    1.0925484305920792,
    -1.0925484305920792,
    0.31539156525252005,
    -1.0925484305920792,
    0.5462742152960396,
)
SH_THREE = (
    -0.5900435899266435,
    2.890611442640554,
    -0.4570457994644658,
    0.3731763325901154,
    -0.4570457994644658,
    1.445305721320277,
    -0.5900435899266435,
)


def harmonics(dir_x, dir_y, dir_z):
    sq_x, sq_y, sq_z = (dir_x * dir_x, dir_y * dir_y, dir_z * dir_z)
    rows = [
        SH_ZERO * jnp.ones_like(dir_x),
        -SH_ONE * dir_y,
        SH_ONE * dir_z,
        -SH_ONE * dir_x,
        SH_TWO[0] * dir_x * dir_y,
        SH_TWO[1] * dir_y * dir_z,
        SH_TWO[2] * (2.0 * sq_z - sq_x - sq_y),
        SH_TWO[3] * dir_x * dir_z,
        SH_TWO[4] * (sq_x - sq_y),
        SH_THREE[0] * dir_y * (3.0 * sq_x - sq_y),
        SH_THREE[1] * dir_x * dir_y * dir_z,
        SH_THREE[2] * dir_y * (4.0 * sq_z - sq_x - sq_y),
        SH_THREE[3] * dir_z * (2.0 * sq_z - 3.0 * sq_x - 3.0 * sq_y),
        SH_THREE[4] * dir_x * (4.0 * sq_z - sq_x - sq_y),
        SH_THREE[5] * dir_z * (sq_x - sq_y),
        SH_THREE[6] * dir_x * (sq_x - 3.0 * sq_y),
    ]
    return rows


def project(table, camera):
    focal_x, focal_y, centre_x, centre_y = camera
    mean_x, mean_y, mean_z = table[0:3]
    spread = [jnp.exp(value) for value in table[3:6]]
    quat = table[6:10]
    length = jnp.sqrt(
        quat[0] * quat[0] + quat[1] * quat[1] + quat[2] * quat[2] + quat[3] * quat[3]
    )
    inverse = 1.0 / length
    w_part, x_part, y_part, z_part = [value * inverse for value in quat]
    rotate = [
        [
            1.0 - 2.0 * (y_part * y_part + z_part * z_part),
            2.0 * (x_part * y_part - w_part * z_part),
            2.0 * (x_part * z_part + w_part * y_part),
        ],
        [
            2.0 * (x_part * y_part + w_part * z_part),
            1.0 - 2.0 * (x_part * x_part + z_part * z_part),
            2.0 * (y_part * z_part - w_part * x_part),
        ],
        [
            2.0 * (x_part * z_part - w_part * y_part),
            2.0 * (y_part * z_part + w_part * x_part),
            1.0 - 2.0 * (x_part * x_part + y_part * y_part),
        ],
    ]
    scaled = [[rotate[row][col] * spread[col] for col in range(3)] for row in range(3)]
    depth_inv = 1.0 / mean_z
    ratio_x = mean_x * depth_inv
    ratio_y = mean_y * depth_inv
    scale_x = focal_x * depth_inv
    scale_y = focal_y * depth_inv
    top = [scale_x * (scaled[0][col] - ratio_x * scaled[2][col]) for col in range(3)]
    low = [scale_y * (scaled[1][col] - ratio_y * scaled[2][col]) for col in range(3)]
    cov_a = top[0] * top[0] + top[1] * top[1] + top[2] * top[2] + 0.3
    cov_b = top[0] * low[0] + top[1] * low[1] + top[2] * low[2]
    cov_c = low[0] * low[0] + low[1] * low[1] + low[2] * low[2] + 0.3
    det_inv = 1.0 / (cov_a * cov_c - cov_b * cov_b)
    screen_x = focal_x * ratio_x + centre_x
    screen_y = focal_y * ratio_y + centre_y
    opacity = 1.0 / (1.0 + jnp.exp(-table[10]))
    radius_inv = 1.0 / jnp.sqrt(mean_x * mean_x + mean_y * mean_y + mean_z * mean_z)
    basis = harmonics(mean_x * radius_inv, mean_y * radius_inv, mean_z * radius_inv)
    colours = []
    for channel in range(3):
        total = table[11 + 16 * channel] * basis[0]
        for term in range(1, 16):
            total = total + table[11 + 16 * channel + term] * basis[term]
        colours.append(jnp.maximum(total + 0.5, 0.0))
    return [
        screen_x,
        screen_y,
        cov_c * det_inv,
        -cov_b * det_inv,
        cov_a * det_inv,
        opacity,
    ] + colours


def halves(first, second):
    lane = lax.broadcasted_iota(jnp.int32, (8, 128), 1)
    top = jnp.where(lane < HALF, first, pltpu.roll(second, HALF, 1))
    low = jnp.where(lane < HALF, pltpu.roll(first, HALF, 1), second)
    return jnp.concatenate([top, low], axis=0)


def packed(block):
    lane = lax.broadcasted_iota(jnp.int32, (8, 128), 1)
    top, low = block[0:8, :], block[8:16, :]
    first = jnp.where(lane < HALF, top, pltpu.roll(low, HALF, 1))
    second = jnp.where(lane < HALF, pltpu.roll(top, HALF, 1), low)
    return first, second


def project_kernel(camera_ref, gauss_ref, tab, feat):
    camera = [camera_ref[k] for k in range(4)]
    feat[...] = jnp.zeros_like(feat)

    @pl.loop(0, gauss_ref.shape[1] // 8)
    def _(slab):
        here = pl.ds(pl.multiple_of(slab * 8, 8), 8)
        values = project([gauss_ref[k, here, :] for k in range(59)], camera)
        u, v, conic_a, conic_b, conic_c, opacity = values[:6]
        sent = [u, v, -0.5 * conic_a, -conic_b, -0.5 * conic_c, opacity] + values[6:]
        for r in range(8):
            lanes = pl.ds(pl.multiple_of(slab * 1024 + r * 128, 128), 128)
            for k in range(9):
                feat[k : k + 1, lanes] = sent[k][r : r + 1, :]

    for block in range(tab.shape[0] // 128):
        lanes = slice(block * 128, block * 128 + 128)
        tab[lanes, 0:PACK] = feat[:, lanes].T


def bring_kernel(
    sizes,
    fetch_ref,
    tab,
    asked_ref,
    table_ref,
    indices,
    rows,
    offered,
    ask_send,
    ask_recv,
    send_sem,
    recv_sem,
    own_sem,
):
    n = sizes[0] * sizes[1]
    bits = sizes[1].bit_length() - 1
    me = (lax.axis_index("tile") << bits) | lax.axis_index("shard")
    shift = (me & 1) * HALF
    barrier = pltpu.get_barrier_semaphore()

    def place(peer):
        return (peer >> bits, peer & (sizes[1] - 1))

    def greet(step, unused):
        peer = (me + step) & (n - 1)
        pl.semaphore_signal(barrier, inc=1, device_id=place(peer), device_id_type=MESH)
        return unused

    def ask(step, unused):
        peer = (me + step) & (n - 1)
        pltpu.make_async_remote_copy(
            src_ref=fetch_ref.at[peer >> 1],
            dst_ref=asked_ref.at[me],
            send_sem=ask_send,
            recv_sem=ask_recv,
            device_id=place(peer),
            device_id_type=MESH,
        ).start()
        return unused

    def give(peer):
        pltpu.make_async_remote_copy(
            src_ref=offered.at[peer],
            dst_ref=table_ref.at[me],
            send_sem=send_sem,
            recv_sem=recv_sem,
            device_id=place(peer),
            device_id_type=MESH,
        ).start()

    def gather(pair):
        for half in range(2):
            for k in range(0, HALF, BATCH):
                picked = [
                    tab[pl.ds(indices[2 * pair + half, 0, shift + k + part], 1), :]
                    for part in range(BATCH)
                ]
                first = half * HALF + k
                rows[first : first + BATCH, :] = jnp.concatenate(picked, axis=0)
        first, second = packed(rows[:, 0:PACK].T)
        offered[2 * pair] = first
        offered[2 * pair + 1] = second

    def serve(step, unused):
        pair = ((me >> 1) + step) & (n // 2 - 1)
        gather(pair)
        give(2 * pair)
        give(2 * pair + 1)
        return unused

    own = pltpu.make_async_copy(fetch_ref.at[me >> 1], asked_ref.at[me], own_sem)
    own.start()
    lax.fori_loop(1, n, greet, 0)
    pl.semaphore_wait(barrier, n - 1)
    lax.fori_loop(1, n, ask, 0)
    own.wait()
    others = asked_ref.at[pl.ds(0, n - 1)]
    pltpu.make_async_copy(others, others, ask_recv).wait()
    inside = pltpu.make_async_copy(asked_ref, indices, own_sem)
    inside.start()
    inside.wait()
    lax.fori_loop(1, n // 2, serve, 0)
    gather(me >> 1)
    give(me ^ 1)
    table_ref[me] = offered[me]
    pltpu.make_async_copy(others, others, ask_send).wait()
    others = table_ref.at[pl.ds(0, n - 1)]
    pltpu.make_async_copy(others, others, send_sem).wait()
    pltpu.make_async_copy(others, others, recv_sem).wait()


def settle_kernel(camera_ref, asked_ref, shift_ref, gauss_ref, moment_ref, out_ref, tab, rows, sums):
    camera = [camera_ref[k] for k in range(4)]
    shift = shift_ref[0]

    @pl.loop(0, moment_ref.shape[0] // 2)
    def _(pair):
        rows[:, 0:PACK] = halves(moment_ref[2 * pair], moment_ref[2 * pair + 1]).T
        for half in range(2):
            for k in range(0, HALF, BATCH):
                first = half * HALF + k
                block = rows[first : first + BATCH, :]
                for part in range(BATCH):
                    place = asked_ref[2 * pair + half, shift + k + part]
                    tab[pl.ds(place, 1), :] = block[part : part + 1, :]

    for block in range(tab.shape[0] // 128):
        lanes = slice(block * 128, block * 128 + 128)
        sums[:, lanes] = tab[lanes, 0:PACK].T

    @pl.loop(0, gauss_ref.shape[1] // 8)
    def _(slab):
        here = pl.ds(pl.multiple_of(slab * 8, 8), 8)

        def moment(k):
            parts = [
                sums[k : k + 1, pl.ds(pl.multiple_of(slab * 1024 + r * 128, 128), 128)]
                for r in range(8)
            ]
            return jnp.concatenate(parts, axis=0)

        values, back = jax.vjp(
            lambda *table: project(list(table), camera),
            *[gauss_ref[k, here, :] for k in range(59)],
        )
        u, v, conic_a, conic_b, conic_c, opacity = values[:6]
        g_0, g_x, g_y, g_xx, g_xy, g_yy = [moment(k) for k in range(6)]
        u = u - moment(11)
        v = v - moment(12)
        s_x = g_x - u * g_0
        s_y = g_y - v * g_0
        s_xx = g_xx - u * (g_x + s_x)
        s_xy = g_xy - u * g_y - v * s_x
        s_yy = g_yy - v * (g_y + s_y)
        given = [
            conic_a * s_x + conic_b * s_y,
            conic_c * s_y + conic_b * s_x,
            -0.5 * s_xx,
            -s_xy,
            -0.5 * s_yy,
            g_0 / opacity,
        ] + [moment(8 + k) for k in range(3)]
        grads = back(given)
        for k in range(59):
            out_ref[k, here, :] = grads[k]


def exchange_kernel(sizes, in_ref, out_ref, send_sem, recv_sem, own_sem):
    n = sizes[0] * sizes[1]
    share = (n // in_ref.shape[0]).bit_length() - 1
    bits = sizes[1].bit_length() - 1
    me = (lax.axis_index("tile") << bits) | lax.axis_index("shard")
    barrier = pltpu.get_barrier_semaphore()

    def place(peer):
        return (peer >> bits, peer & (sizes[1] - 1))

    def greet(step, unused):
        peer = (me + step) & (n - 1)
        pl.semaphore_signal(barrier, inc=1, device_id=place(peer), device_id_type=MESH)
        return unused

    def start(step, unused):
        peer = (me + step) & (n - 1)
        pltpu.make_async_remote_copy(
            src_ref=in_ref.at[peer >> share],
            dst_ref=out_ref.at[me],
            send_sem=send_sem,
            recv_sem=recv_sem,
            device_id=place(peer),
            device_id_type=MESH,
        ).start()
        return unused

    own = pltpu.make_async_copy(in_ref.at[me >> share], out_ref.at[me], own_sem)
    own.start()
    lax.fori_loop(1, n, greet, 0)
    pl.semaphore_wait(barrier, n - 1)
    lax.fori_loop(1, n, start, 0)
    own.wait()
    others = out_ref.at[pl.ds(0, n - 1)]
    pltpu.make_async_copy(others, others, send_sem).wait()
    pltpu.make_async_copy(others, others, recv_sem).wait()


def exchange(blocks, sizes, number, name):
    n = sizes[0] * sizes[1]
    return pl.pallas_call(
        functools.partial(exchange_kernel, sizes),
        out_shape=jax.ShapeDtypeStruct((n,) + blocks.shape[1:], blocks.dtype),
        in_specs=[pl.BlockSpec(memory_space=pltpu.VMEM)],
        out_specs=pl.BlockSpec(memory_space=pltpu.VMEM),
        scratch_shapes=[
            pltpu.SemaphoreType.DMA,
            pltpu.SemaphoreType.DMA,
            pltpu.SemaphoreType.DMA,
        ],
        compiler_params=pltpu.CompilerParams(collective_id=number, has_side_effects=True),
        name=name,
    )(blocks)


def split(value):
    high = value.astype(jnp.bfloat16)
    return high, (value - high.astype(jnp.float32)).astype(jnp.bfloat16)


def times(left, right, dims):
    return lax.dot_general(left, right, dims, preferred_element_type=jnp.float32)


def render_kernel(
    ids_ref,
    counts_ref,
    active_ref,
    lists_ref,
    feat_ref,
    target_ref,
    pixel_ref,
    mono_ref,
    image_ref,
    out_ref,
    tab,
    line,
    rows,
    alphas,
    weights,
    powers,
    errors,
):
    need = feat_ref.shape[0] * HALF
    span = need // SEGMENTS
    slots = image_ref.shape[1]
    lane = lax.broadcasted_iota(jnp.int32, (1, 128), 1)

    for block in range(need // 128):
        lanes = slice(block * 128, block * 128 + 128)
        values = halves(feat_ref[2 * block], feat_ref[2 * block + 1])
        colours = [jnp.broadcast_to(values[6 + k : 7 + k, :], (16, 128)) for k in range(3)]
        tab[lanes, 0:WIDE] = jnp.concatenate([values] + colours, axis=0).T

    def centre(slot):
        tile = ids_ref[slot]
        centre_x = ((tile % TILES_X) * TILE_SIDE + TILE_SIDE // 2).astype(jnp.float32)
        centre_y = ((tile // TILES_X) * TILE_SIDE + TILE_SIDE // 2).astype(jnp.float32)
        return centre_x, centre_y

    def of_tile(slot):
        return (lane >= 16) & (lane < WIDE) & (lane % 16 == slot)

    def pick(slot, start):
        count = counts_ref[slot]
        centre_x, centre_y = centre(slot)
        alive = jnp.where(active_ref[slot] > 0, 1.0, 0.0)
        scale = jnp.where((lane < 5) | of_tile(slot), 1.0, jnp.where(lane == 5, alive, 0.0))
        offset = jnp.where(lane == 0, -centre_x, jnp.where(lane == 1, -centre_y, 0.0))
        offset = jnp.where(lane == 6, start.astype(jnp.float32), offset)
        offset = jnp.where(lane == 7, (start + count).astype(jnp.float32), offset)

        @pl.loop(0, (count + BATCH - 1) // BATCH)
        def _(step):
            first = step * BATCH
            picked = [
                tab[pl.ds(lists_ref[slot, first + part], 1), :] for part in range(BATCH)
            ]
            block = jnp.concatenate(picked, axis=0) * scale + offset
            line[pl.ds(start + first, BATCH), :] = block

        return start + count

    lax.fori_loop(0, slots, pick, jnp.int32(0))
    for segment in range(SEGMENTS):
        whole = slice(segment * span, segment * span + span)
        rows[pl.ds(segment, span, stride=SEGMENTS), :] = line[whole, :]

    pixel_x = jnp.broadcast_to(pixel_ref[0:1, :], (8, PIXELS))
    pixel_y = jnp.broadcast_to(pixel_ref[1:2, :], (8, PIXELS))
    sets = range(SEGMENTS // 8)
    sub = lax.broadcasted_iota(jnp.int32, (8, 1), 0)
    bases = [((sub + 8 * q) * span).astype(jnp.float32) for q in sets]
    one = jnp.ones((8, PIXELS), jnp.float32)
    zero = jnp.zeros((8, PIXELS), jnp.float32)

    def forward(step, state):
        left, seen = list(state[0]), list(state[1])
        for part in range(STEPS):
            place = step * STEPS + part
            for q in sets:
                here = pl.ds(pl.multiple_of(place * SEGMENTS + 8 * q, 8), 8)
                row = rows[here, :]
                delta_x = pixel_x - row[:, 0:1]
                delta_y = pixel_y - row[:, 1:2]
                power = (
                    delta_x * (row[:, 2:3] * delta_x + row[:, 3:4] * delta_y)
                    + row[:, 4:5] * delta_y * delta_y
                )
                alpha = row[:, 5:6] * jnp.exp(power)
                begins = jnp.where(row[:, 6:7] == bases[q] + place.astype(jnp.float32), 1.0, 0.0)
                seen[q] = jnp.maximum(seen[q], begins)
                passed = jnp.where(jnp.broadcast_to(begins, (8, PIXELS)) > 0.0, 1.0, left[q])
                alphas[here, :] = alpha
                weights[here, :] = alpha * passed
                left[q] = passed * (1.0 - alpha)
        return tuple(left), tuple(seen)

    none = jnp.zeros((8, 1), jnp.float32)
    left, seen = lax.fori_loop(
        0, span // STEPS, forward, (tuple(one for q in sets), tuple(none for q in sets))
    )
    carry = one[0:1, :]
    ahead = []
    for q in sets:
        parts = []
        for k in range(8):
            parts.append(carry)
            begun = seen[q][k : k + 1, :]
            carry = left[q][k : k + 1, :] * (begun + (1.0 - begun) * carry)
        ahead.append(jnp.concatenate(parts, axis=0))

    def composite(chunk, image):
        here = pl.ds(pl.multiple_of(chunk * CHUNK, CHUNK), CHUNK)
        for group in range(CHUNK // 8):
            q = group % len(sets)
            part = pl.ds(pl.multiple_of(chunk * CHUNK + 8 * group, 8), 8)
            head = jnp.where(rows[part, 6:7] < bases[q], 1.0, 0.0)
            factor = jnp.where(jnp.broadcast_to(head, (8, PIXELS)) > 0.0, ahead[q], 1.0)
            weights[part, :] = weights[part, :] * factor
        colour_high, colour_low = split(rows[here, 0:WIDE].T)
        weight_high, weight_low = split(weights[here, :])
        return (
            image
            + times(colour_low, weight_high, NN)
            + times(colour_high, weight_low, NN)
            + times(colour_high, weight_high, NN)
        )

    chunks = need // CHUNK
    image = lax.fori_loop(0, chunks, composite, jnp.zeros((WIDE, PIXELS), jnp.float32))
    errors[0:16, :] = jnp.zeros((16, PIXELS), jnp.float32)
    for k in range(3):
        part = image[16 + 16 * k : 32 + 16 * k, :]
        image_ref[k] = part
        errors[16 + 16 * k : 32 + 16 * k, :] = part - target_ref[k]

    def backward(step, later):
        later = list(later)
        chunk = chunks - 1 - step
        here = pl.ds(pl.multiple_of(chunk * CHUNK, CHUNK), CHUNK)
        colour_high, colour_low = split(rows[here, 0:WIDE])
        error_high, error_low = split(errors[...])
        powers[here, :] = (
            times(colour_low, error_high, NN)
            + times(colour_high, error_low, NN)
            + times(colour_high, error_high, NN)
        )
        for group in reversed(range(CHUNK // 8)):
            q = group % len(sets)
            part = pl.ds(pl.multiple_of(chunk * CHUNK + 8 * group, 8), 8)
            after = (chunk * (CHUNK // SEGMENTS) + group // len(sets) + 1).astype(jnp.float32)
            ends = jnp.where(rows[part, 7:8] == bases[q] + after, 1.0, 0.0)
            alpha = alphas[part, :]
            given = weights[part, :] * powers[part, :]
            rest = jnp.where(jnp.broadcast_to(ends, (8, PIXELS)) > 0.0, 0.0, later[q])
            ratio = alpha / (1.0 - alpha)
            alphas[part, :] = ratio
            powers[part, :] = given - ratio * rest
            later[q] = rest + given
        return tuple(later)

    later = lax.fori_loop(0, chunks, backward, tuple(zero for q in sets))
    carry = zero[0:1, :]
    behind = []
    for q in reversed(sets):
        final = pl.ds((span - 1) * SEGMENTS + 8 * q, 8)
        onward = jnp.where(rows[final, 7:8] > bases[q] + span, 1.0, 0.0) * (1.0 - seen[q])
        parts = []
        for k in reversed(range(8)):
            parts.append(carry)
            carry = later[q][k : k + 1, :] + onward[k : k + 1, :] * carry
        behind.append(jnp.concatenate(parts[::-1], axis=0))
    behind = behind[::-1]

    @pl.loop(0, chunks)
    def _(chunk):
        here = pl.ds(pl.multiple_of(chunk * CHUNK, CHUNK), CHUNK)
        for group in range(CHUNK // 8):
            q = group % len(sets)
            part = pl.ds(pl.multiple_of(chunk * CHUNK + 8 * group, 8), 8)
            tail = jnp.where(rows[part, 7:8] > bases[q] + span, 1.0, 0.0)
            rest = jnp.where(jnp.broadcast_to(tail, (8, PIXELS)) > 0.0, behind[q], 0.0)
            powers[part, :] = powers[part, :] - alphas[part, :] * rest
        power_high, power_low = split(powers[here, :])
        weight_high, weight_low = split(weights[here, :])
        error_high, error_low = split(errors[...])
        mono = mono_ref[...].astype(jnp.bfloat16)
        rows[here, 0:WIDE] = (
            times(power_low, mono, NT)
            + times(weight_low, error_high, NT)
            + times(weight_high, error_low, NT)
            + times(power_high, mono, NT)
            + times(weight_high, error_high, NT)
        )

    for segment in range(SEGMENTS):
        whole = slice(segment * span, segment * span + span)
        line[whole, :] = rows[pl.ds(segment, span, stride=SEGMENTS), :]

    def put(slot, start):
        count = counts_ref[slot]
        centre_x, centre_y = centre(slot)
        scale = jnp.where((lane < 6) | of_tile(slot), 1.0, 0.0)
        offset = jnp.where(lane == 11, centre_x, jnp.where(lane == 12, centre_y, 0.0))

        @pl.loop(0, (count + BATCH - 1) // BATCH)
        def _(step):
            first = step * BATCH
            block = line[pl.ds(start + first, BATCH), :] * scale + offset
            for part in range(BATCH):
                place = lists_ref[slot, first + part]
                place = jnp.where(first + part < count, place, need)
                tab[pl.ds(place, 1), :] = block[part : part + 1, :]

        return start + count

    lax.fori_loop(0, slots, put, jnp.int32(0))
    sub = lax.broadcasted_iota(jnp.int32, (8, 128), 0)
    for block in range(need // 128):
        lanes = slice(block * 128, block * 128 + 128)
        values = tab[lanes, 0:WIDE].T
        low = values[8:16, :]
        for k in range(3):
            summed = jnp.sum(values[16 + 16 * k : 32 + 16 * k, :], axis=0, keepdims=True)
            low = jnp.where(sub == k, summed, low)
        first, second = packed(jnp.concatenate([values[0:8, :], low], axis=0))
        out_ref[2 * block] = first
        out_ref[2 * block + 1] = second


def render(features, tiles, lists, counts, active, target):
    need = features.shape[0] * HALF
    if target.shape[1] != 16 or need % (SEGMENTS * 128) != 0:
        raise ValueError("unsupported sizes")
    spot = np.arange(PIXELS)
    local_x = spot % TILE_SIDE + 0.5 - TILE_SIDE // 2
    local_y = spot // TILE_SIDE + 0.5 - TILE_SIDE // 2
    pixel = np.zeros((8, PIXELS), np.float32)
    pixel[0], pixel[1] = local_x, local_y
    mono = np.zeros((WIDE, PIXELS), np.float32)
    mono[0] = 1.0
    mono[1], mono[2] = local_x, local_y
    mono[3], mono[4], mono[5] = local_x * local_x, local_x * local_y, local_y * local_y
    smem = pl.BlockSpec(memory_space=pltpu.SMEM)
    vmem = pl.BlockSpec(memory_space=pltpu.VMEM)
    return pl.pallas_call(
        render_kernel,
        out_shape=(
            jax.ShapeDtypeStruct(target.shape, jnp.float32),
            jax.ShapeDtypeStruct(features.shape, jnp.float32),
        ),
        in_specs=[smem] * 4 + [vmem] * 4,
        out_specs=(vmem, vmem),
        scratch_shapes=[
            pltpu.VMEM((need + 8, 128), jnp.float32),
            pltpu.VMEM((need + BATCH, 128), jnp.float32),
            pltpu.VMEM((need, 128), jnp.float32),
            pltpu.VMEM((need, PIXELS), jnp.float32),
            pltpu.VMEM((need, PIXELS), jnp.float32),
            pltpu.VMEM((need, PIXELS), jnp.float32),
            pltpu.VMEM((WIDE, PIXELS), jnp.float32),
        ],
        compiler_params=pltpu.CompilerParams(vmem_limit_bytes=48 * 1024 * 1024),
        name="render",
    )(tiles, counts, active, lists, features, target, jnp.asarray(pixel), jnp.asarray(mono))


def per_device(
    sizes,
    gaussians,
    camera,
    fetch_index,
    tile_ids,
    tile_lists,
    tile_counts,
    tile_active,
    target,
):
    owned = gaussians.shape[1]
    need = fetch_index.shape[1]
    n = sizes[0] * sizes[1]
    if sizes[1] & (sizes[1] - 1) or n & (n - 1):
        raise ValueError("unsupported mesh")
    if need != n * HALF or owned % 1024 != 0:
        raise ValueError("unsupported sizes")
    smem = pl.BlockSpec(memory_space=pltpu.SMEM)
    vmem = pl.BlockSpec(memory_space=pltpu.VMEM)
    slabs = gaussians.reshape(59, owned // 128, 128)
    params = pltpu.CompilerParams(vmem_limit_bytes=40 * 1024 * 1024)
    me = lax.axis_index("tile") * sizes[1] + lax.axis_index("shard")
    shift = (lax.rem(me, 2) * HALF).astype(jnp.int32).reshape(1)
    features = pl.pallas_call(
        project_kernel,
        out_shape=jax.ShapeDtypeStruct((owned, 128), jnp.float32),
        in_specs=[smem, vmem],
        out_specs=vmem,
        scratch_shapes=[pltpu.VMEM((PACK, owned), jnp.float32)],
        compiler_params=params,
        name="project",
    )(camera, slabs)
    asked, table = pl.pallas_call(
        functools.partial(bring_kernel, sizes),
        out_shape=(
            jax.ShapeDtypeStruct((n, 1, 128), jnp.int32),
            jax.ShapeDtypeStruct((n, 8, 128), jnp.float32),
        ),
        in_specs=[vmem, vmem],
        out_specs=(vmem, vmem),
        scratch_shapes=[
            pltpu.SMEM((n, 1, 128), jnp.int32),
            pltpu.VMEM((128, 128), jnp.float32),
            pltpu.VMEM((n, 8, 128), jnp.float32),
        ]
        + [pltpu.SemaphoreType.DMA] * 5,
        compiler_params=pltpu.CompilerParams(
            collective_id=0, has_side_effects=True, vmem_limit_bytes=40 * 1024 * 1024
        ),
        name="bring",
    )(fetch_index.reshape(n // 2, 1, 128), features)
    asked = asked.reshape(n, 128)
    image, moments = render(
        table, tile_ids[0], tile_lists[0], tile_counts[0], tile_active[0], target
    )
    returned = exchange(moments, sizes, 2, "give")
    grads = pl.pallas_call(
        settle_kernel,
        out_shape=jax.ShapeDtypeStruct(slabs.shape, jnp.float32),
        in_specs=[smem, smem, smem, vmem, vmem],
        out_specs=vmem,
        scratch_shapes=[
            pltpu.VMEM((owned, 128), jnp.float32),
            pltpu.VMEM((128, 128), jnp.float32),
            pltpu.VMEM((PACK, owned), jnp.float32),
        ],
        compiler_params=params,
        name="settle",
    )(camera, asked, shift, slabs, returned)
    return (image, grads.reshape(gaussians.shape))


def solution(mesh):
    in_specs = (
        P(None, ("tile", "shard")),
        P(),
        P(("tile", "shard"), None),
        P(("tile", "shard"), None),
        P(("tile", "shard"), None, None),
        P(("tile", "shard"), None),
        P(("tile", "shard"), None),
        P(None, ("tile", "shard"), None),
    )
    out_specs = (P(None, ("tile", "shard"), None), P(None, ("tile", "shard")))
    sizes = (mesh.shape["tile"], mesh.shape["shard"])
    return jax.shard_map(
        functools.partial(per_device, sizes), mesh=mesh, in_specs=in_specs, out_specs=out_specs, check_vma=False
    )
```

```python
import functools

import jax
import jax.numpy as jnp
import numpy as np
from jax import lax
from jax.experimental import pallas as pl
from jax.experimental.pallas import tpu as pltpu
from jax.sharding import PartitionSpec as P

TILE_SIDE = 16
TILES_X = 64
PIXELS = TILE_SIDE * TILE_SIDE
PACK = 16
HALF = 64
WIDE = 64
SEGMENTS = 16
STEPS = 16
BATCH = 16
CHUNK = 256
NN = (((1,), (0,)), ((), ()))
NT = (((1,), (1,)), ((), ()))
MESH = pl.DeviceIdType.MESH


SH_ZERO = 0.28209479177387814
SH_ONE = 0.4886025119029199
SH_TWO = (
    1.0925484305920792,
    -1.0925484305920792,
    0.31539156525252005,
    -1.0925484305920792,
    0.5462742152960396,
)
SH_THREE = (
    -0.5900435899266435,
    2.890611442640554,
    -0.4570457994644658,
    0.3731763325901154,
    -0.4570457994644658,
    1.445305721320277,
    -0.5900435899266435,
)


def harmonics(dir_x, dir_y, dir_z):
    sq_x, sq_y, sq_z = (dir_x * dir_x, dir_y * dir_y, dir_z * dir_z)
    rows = [
        SH_ZERO * jnp.ones_like(dir_x),
        -SH_ONE * dir_y,
        SH_ONE * dir_z,
        -SH_ONE * dir_x,
        SH_TWO[0] * dir_x * dir_y,
        SH_TWO[1] * dir_y * dir_z,
        SH_TWO[2] * (2.0 * sq_z - sq_x - sq_y),
        SH_TWO[3] * dir_x * dir_z,
        SH_TWO[4] * (sq_x - sq_y),
        SH_THREE[0] * dir_y * (3.0 * sq_x - sq_y),
        SH_THREE[1] * dir_x * dir_y * dir_z,
        SH_THREE[2] * dir_y * (4.0 * sq_z - sq_x - sq_y),
        SH_THREE[3] * dir_z * (2.0 * sq_z - 3.0 * sq_x - 3.0 * sq_y),
        SH_THREE[4] * dir_x * (4.0 * sq_z - sq_x - sq_y),
        SH_THREE[5] * dir_z * (sq_x - sq_y),
        SH_THREE[6] * dir_x * (sq_x - 3.0 * sq_y),
    ]
    return rows


def project(table, camera):
    focal_x, focal_y, centre_x, centre_y = camera
    mean_x, mean_y, mean_z = table[0:3]
    spread = [jnp.exp(value) for value in table[3:6]]
    quat = table[6:10]
    length = jnp.sqrt(
        quat[0] * quat[0] + quat[1] * quat[1] + quat[2] * quat[2] + quat[3] * quat[3]
    )
    inverse = 1.0 / length
    w_part, x_part, y_part, z_part = [value * inverse for value in quat]
    rotate = [
        [
            1.0 - 2.0 * (y_part * y_part + z_part * z_part),
            2.0 * (x_part * y_part - w_part * z_part),
            2.0 * (x_part * z_part + w_part * y_part),
        ],
        [
            2.0 * (x_part * y_part + w_part * z_part),
            1.0 - 2.0 * (x_part * x_part + z_part * z_part),
            2.0 * (y_part * z_part - w_part * x_part),
        ],
        [
            2.0 * (x_part * z_part - w_part * y_part),
            2.0 * (y_part * z_part + w_part * x_part),
            1.0 - 2.0 * (x_part * x_part + y_part * y_part),
        ],
    ]
    scaled = [[rotate[row][col] * spread[col] for col in range(3)] for row in range(3)]
    depth_inv = 1.0 / mean_z
    ratio_x = mean_x * depth_inv
    ratio_y = mean_y * depth_inv
    scale_x = focal_x * depth_inv
    scale_y = focal_y * depth_inv
    top = [scale_x * (scaled[0][col] - ratio_x * scaled[2][col]) for col in range(3)]
    low = [scale_y * (scaled[1][col] - ratio_y * scaled[2][col]) for col in range(3)]
    cov_a = top[0] * top[0] + top[1] * top[1] + top[2] * top[2] + 0.3
    cov_b = top[0] * low[0] + top[1] * low[1] + top[2] * low[2]
    cov_c = low[0] * low[0] + low[1] * low[1] + low[2] * low[2] + 0.3
    det_inv = 1.0 / (cov_a * cov_c - cov_b * cov_b)
    screen_x = focal_x * ratio_x + centre_x
    screen_y = focal_y * ratio_y + centre_y
    opacity = 1.0 / (1.0 + jnp.exp(-table[10]))
    radius_inv = 1.0 / jnp.sqrt(mean_x * mean_x + mean_y * mean_y + mean_z * mean_z)
    basis = harmonics(mean_x * radius_inv, mean_y * radius_inv, mean_z * radius_inv)
    colours = []
    for channel in range(3):
        total = table[11 + 16 * channel] * basis[0]
        for term in range(1, 16):
            total = total + table[11 + 16 * channel + term] * basis[term]
        colours.append(jnp.maximum(total + 0.5, 0.0))
    return [
        screen_x,
        screen_y,
        cov_c * det_inv,
        -cov_b * det_inv,
        cov_a * det_inv,
        opacity,
    ] + colours


def halves(first, second):
    lane = lax.broadcasted_iota(jnp.int32, (8, 128), 1)
    top = jnp.where(lane < HALF, first, pltpu.roll(second, HALF, 1))
    low = jnp.where(lane < HALF, pltpu.roll(first, HALF, 1), second)
    return jnp.concatenate([top, low], axis=0)


def packed(block):
    lane = lax.broadcasted_iota(jnp.int32, (8, 128), 1)
    top, low = block[0:8, :], block[8:16, :]
    first = jnp.where(lane < HALF, top, pltpu.roll(low, HALF, 1))
    second = jnp.where(lane < HALF, pltpu.roll(top, HALF, 1), low)
    return first, second


def project_kernel(camera_ref, gauss_ref, tab, feat):
    camera = [camera_ref[k] for k in range(4)]
    feat[...] = jnp.zeros_like(feat)

    @pl.loop(0, gauss_ref.shape[1] // 8)
    def _(slab):
        here = pl.ds(pl.multiple_of(slab * 8, 8), 8)
        values = project([gauss_ref[k, here, :] for k in range(59)], camera)
        u, v, conic_a, conic_b, conic_c, opacity = values[:6]
        sent = [u, v, -0.5 * conic_a, -conic_b, -0.5 * conic_c, opacity] + values[6:]
        for r in range(8):
            lanes = pl.ds(pl.multiple_of(slab * 1024 + r * 128, 128), 128)
            for k in range(9):
                feat[k : k + 1, lanes] = sent[k][r : r + 1, :]

    for block in range(tab.shape[0] // 128):
        lanes = slice(block * 128, block * 128 + 128)
        tab[lanes, 0:PACK] = feat[:, lanes].T


def bring_kernel(
    sizes,
    fetch_ref,
    tab,
    asked_ref,
    table_ref,
    indices,
    rows,
    offered,
    ask_send,
    ask_recv,
    send_sem,
    recv_sem,
    own_sem,
):
    n = sizes[0] * sizes[1]
    bits = sizes[1].bit_length() - 1
    me = (lax.axis_index("tile") << bits) | lax.axis_index("shard")
    shift = (me & 1) * HALF
    barrier = pltpu.get_barrier_semaphore()

    def place(peer):
        return (peer >> bits, peer & (sizes[1] - 1))

    def greet(step, unused):
        peer = (me + step) & (n - 1)
        pl.semaphore_signal(barrier, inc=1, device_id=place(peer), device_id_type=MESH)
        return unused

    def ask(step, unused):
        peer = (me + step) & (n - 1)
        pltpu.make_async_remote_copy(
            src_ref=fetch_ref.at[peer >> 1],
            dst_ref=asked_ref.at[me],
            send_sem=ask_send,
            recv_sem=ask_recv,
            device_id=place(peer),
            device_id_type=MESH,
        ).start()
        return unused

    def give(peer):
        pltpu.make_async_remote_copy(
            src_ref=offered.at[peer],
            dst_ref=table_ref.at[me],
            send_sem=send_sem,
            recv_sem=recv_sem,
            device_id=place(peer),
            device_id_type=MESH,
        ).start()

    def gather(pair):
        for half in range(2):
            for k in range(0, HALF, BATCH):
                picked = [
                    tab[pl.ds(indices[2 * pair + half, 0, shift + k + part], 1), :]
                    for part in range(BATCH)
                ]
                first = half * HALF + k
                rows[first : first + BATCH, :] = jnp.concatenate(picked, axis=0)
        first, second = packed(rows[:, 0:PACK].T)
        offered[2 * pair] = first
        offered[2 * pair + 1] = second

    def serve(step, unused):
        pair = ((me >> 1) + step) & (n // 2 - 1)
        gather(pair)
        give(2 * pair)
        give(2 * pair + 1)
        return unused

    own = pltpu.make_async_copy(fetch_ref.at[me >> 1], asked_ref.at[me], own_sem)
    own.start()
    lax.fori_loop(1, n, greet, 0)
    pl.semaphore_wait(barrier, n - 1)
    lax.fori_loop(1, n, ask, 0)
    own.wait()
    others = asked_ref.at[pl.ds(0, n - 1)]
    pltpu.make_async_copy(others, others, ask_recv).wait()
    inside = pltpu.make_async_copy(asked_ref, indices, own_sem)
    inside.start()
    inside.wait()
    lax.fori_loop(1, n // 2, serve, 0)
    gather(me >> 1)
    give(me ^ 1)
    table_ref[me] = offered[me]
    pltpu.make_async_copy(others, others, ask_send).wait()
    others = table_ref.at[pl.ds(0, n - 1)]
    pltpu.make_async_copy(others, others, send_sem).wait()
    pltpu.make_async_copy(others, others, recv_sem).wait()


def settle_kernel(camera_ref, asked_ref, shift_ref, gauss_ref, moment_ref, out_ref, tab, rows, sums):
    camera = [camera_ref[k] for k in range(4)]
    shift = shift_ref[0]

    @pl.loop(0, moment_ref.shape[0] // 2)
    def _(pair):
        rows[:, 0:PACK] = halves(moment_ref[2 * pair], moment_ref[2 * pair + 1]).T
        for half in range(2):
            for k in range(0, HALF, BATCH):
                first = half * HALF + k
                picked = [rows[first + part : first + part + 1, :] for part in range(BATCH)]
                for part in range(BATCH):
                    place = asked_ref[2 * pair + half, shift + k + part]
                    tab[pl.ds(place, 1), :] = picked[part]

    for block in range(tab.shape[0] // 128):
        lanes = slice(block * 128, block * 128 + 128)
        sums[:, lanes] = tab[lanes, 0:PACK].T

    @pl.loop(0, gauss_ref.shape[1] // 8)
    def _(slab):
        here = pl.ds(pl.multiple_of(slab * 8, 8), 8)

        def moment(k):
            parts = [
                sums[k : k + 1, pl.ds(pl.multiple_of(slab * 1024 + r * 128, 128), 128)]
                for r in range(8)
            ]
            return jnp.concatenate(parts, axis=0)

        values, back = jax.vjp(
            lambda *table: project(list(table), camera),
            *[gauss_ref[k, here, :] for k in range(59)],
        )
        u, v, conic_a, conic_b, conic_c, opacity = values[:6]
        g_0, g_x, g_y, g_xx, g_xy, g_yy = [moment(k) for k in range(6)]
        u = u - moment(11)
        v = v - moment(12)
        s_x = g_x - u * g_0
        s_y = g_y - v * g_0
        s_xx = g_xx - u * (g_x + s_x)
        s_xy = g_xy - u * g_y - v * s_x
        s_yy = g_yy - v * (g_y + s_y)
        given = [
            conic_a * s_x + conic_b * s_y,
            conic_c * s_y + conic_b * s_x,
            -0.5 * s_xx,
            -s_xy,
            -0.5 * s_yy,
            g_0 / opacity,
        ] + [moment(8 + k) for k in range(3)]
        grads = back(given)
        for k in range(59):
            out_ref[k, here, :] = grads[k]


def exchange_kernel(sizes, in_ref, out_ref, send_sem, recv_sem, own_sem):
    n = sizes[0] * sizes[1]
    share = (n // in_ref.shape[0]).bit_length() - 1
    bits = sizes[1].bit_length() - 1
    me = (lax.axis_index("tile") << bits) | lax.axis_index("shard")
    barrier = pltpu.get_barrier_semaphore()

    def place(peer):
        return (peer >> bits, peer & (sizes[1] - 1))

    def greet(step, unused):
        peer = (me + step) & (n - 1)
        pl.semaphore_signal(barrier, inc=1, device_id=place(peer), device_id_type=MESH)
        return unused

    def start(step, unused):
        peer = (me + step) & (n - 1)
        pltpu.make_async_remote_copy(
            src_ref=in_ref.at[peer >> share],
            dst_ref=out_ref.at[me],
            send_sem=send_sem,
            recv_sem=recv_sem,
            device_id=place(peer),
            device_id_type=MESH,
        ).start()
        return unused

    own = pltpu.make_async_copy(in_ref.at[me >> share], out_ref.at[me], own_sem)
    own.start()
    lax.fori_loop(1, n, greet, 0)
    pl.semaphore_wait(barrier, n - 1)
    lax.fori_loop(1, n, start, 0)
    own.wait()
    others = out_ref.at[pl.ds(0, n - 1)]
    pltpu.make_async_copy(others, others, send_sem).wait()
    pltpu.make_async_copy(others, others, recv_sem).wait()


def exchange(blocks, sizes, number, name):
    n = sizes[0] * sizes[1]
    return pl.pallas_call(
        functools.partial(exchange_kernel, sizes),
        out_shape=jax.ShapeDtypeStruct((n,) + blocks.shape[1:], blocks.dtype),
        in_specs=[pl.BlockSpec(memory_space=pltpu.VMEM)],
        out_specs=pl.BlockSpec(memory_space=pltpu.VMEM),
        scratch_shapes=[
            pltpu.SemaphoreType.DMA,
            pltpu.SemaphoreType.DMA,
            pltpu.SemaphoreType.DMA,
        ],
        compiler_params=pltpu.CompilerParams(collective_id=number, has_side_effects=True),
        name=name,
    )(blocks)


def split(value):
    high = value.astype(jnp.bfloat16)
    return high, (value - high.astype(jnp.float32)).astype(jnp.bfloat16)


def times(left, right, dims):
    return lax.dot_general(left, right, dims, preferred_element_type=jnp.float32)


def render_kernel(
    ids_ref,
    counts_ref,
    active_ref,
    lists_ref,
    feat_ref,
    target_ref,
    pixel_ref,
    mono_ref,
    image_ref,
    out_ref,
    tab,
    line,
    rows,
    alphas,
    weights,
    powers,
    errors,
):
    need = feat_ref.shape[0] * HALF
    span = need // SEGMENTS
    slots = image_ref.shape[1]
    lane = lax.broadcasted_iota(jnp.int32, (1, 128), 1)

    for block in range(need // 128):
        lanes = slice(block * 128, block * 128 + 128)
        values = halves(feat_ref[2 * block], feat_ref[2 * block + 1])
        colours = [jnp.broadcast_to(values[6 + k : 7 + k, :], (16, 128)) for k in range(3)]
        tab[lanes, 0:WIDE] = jnp.concatenate([values] + colours, axis=0).T

    def centre(slot):
        tile = ids_ref[slot]
        centre_x = ((tile % TILES_X) * TILE_SIDE + TILE_SIDE // 2).astype(jnp.float32)
        centre_y = ((tile // TILES_X) * TILE_SIDE + TILE_SIDE // 2).astype(jnp.float32)
        return centre_x, centre_y

    def of_tile(slot):
        return (lane >= 16) & (lane < WIDE) & (lane % 16 == slot)

    def pick(slot, start):
        count = counts_ref[slot]
        centre_x, centre_y = centre(slot)
        alive = jnp.where(active_ref[slot] > 0, 1.0, 0.0)
        scale = jnp.where((lane < 5) | of_tile(slot), 1.0, jnp.where(lane == 5, alive, 0.0))
        offset = jnp.where(lane == 0, -centre_x, jnp.where(lane == 1, -centre_y, 0.0))
        offset = jnp.where(lane == 6, start.astype(jnp.float32), offset)
        offset = jnp.where(lane == 7, (start + count).astype(jnp.float32), offset)

        @pl.loop(0, (count + BATCH - 1) // BATCH)
        def _(step):
            first = step * BATCH
            picked = [
                tab[pl.ds(lists_ref[slot, first + part], 1), :] for part in range(BATCH)
            ]
            block = jnp.concatenate(picked, axis=0) * scale + offset
            line[pl.ds(start + first, BATCH), :] = block

        return start + count

    lax.fori_loop(0, slots, pick, jnp.int32(0))
    for segment in range(SEGMENTS):
        whole = slice(segment * span, segment * span + span)
        rows[pl.ds(segment, span, stride=SEGMENTS), :] = line[whole, :]

    pixel_x = jnp.broadcast_to(pixel_ref[0:1, :], (8, PIXELS))
    pixel_y = jnp.broadcast_to(pixel_ref[1:2, :], (8, PIXELS))
    sets = range(SEGMENTS // 8)
    sub = lax.broadcasted_iota(jnp.int32, (8, 1), 0)
    bases = [((sub + 8 * q) * span).astype(jnp.float32) for q in sets]
    one = jnp.ones((8, PIXELS), jnp.float32)
    zero = jnp.zeros((8, PIXELS), jnp.float32)

    def forward(step, state):
        left, seen = list(state[0]), list(state[1])
        for part in range(STEPS):
            place = step * STEPS + part
            for q in sets:
                here = pl.ds(pl.multiple_of(place * SEGMENTS + 8 * q, 8), 8)
                row = rows[here, :]
                delta_x = pixel_x - row[:, 0:1]
                delta_y = pixel_y - row[:, 1:2]
                power = (
                    delta_x * (row[:, 2:3] * delta_x + row[:, 3:4] * delta_y)
                    + row[:, 4:5] * delta_y * delta_y
                )
                alpha = row[:, 5:6] * jnp.exp(power)
                begins = jnp.where(row[:, 6:7] == bases[q] + place.astype(jnp.float32), 1.0, 0.0)
                seen[q] = jnp.maximum(seen[q], begins)
                passed = jnp.where(jnp.broadcast_to(begins, (8, PIXELS)) > 0.0, 1.0, left[q])
                alphas[here, :] = alpha
                weights[here, :] = alpha * passed
                left[q] = passed * (1.0 - alpha)
        return tuple(left), tuple(seen)

    none = jnp.zeros((8, 1), jnp.float32)
    left, seen = lax.fori_loop(
        0, span // STEPS, forward, (tuple(one for q in sets), tuple(none for q in sets))
    )
    carry = one[0:1, :]
    ahead = []
    for q in sets:
        parts = []
        for k in range(8):
            parts.append(carry)
            begun = seen[q][k : k + 1, :]
            carry = left[q][k : k + 1, :] * (begun + (1.0 - begun) * carry)
        ahead.append(jnp.concatenate(parts, axis=0))

    def composite(chunk, image):
        here = pl.ds(pl.multiple_of(chunk * CHUNK, CHUNK), CHUNK)
        for group in range(CHUNK // 8):
            q = group % len(sets)
            part = pl.ds(pl.multiple_of(chunk * CHUNK + 8 * group, 8), 8)
            head = jnp.where(rows[part, 6:7] < bases[q], 1.0, 0.0)
            factor = jnp.where(jnp.broadcast_to(head, (8, PIXELS)) > 0.0, ahead[q], 1.0)
            weights[part, :] = weights[part, :] * factor
        colour_high, colour_low = split(rows[here, 0:WIDE].T)
        weight_high, weight_low = split(weights[here, :])
        return (
            image
            + times(colour_low, weight_high, NN)
            + times(colour_high, weight_low, NN)
            + times(colour_high, weight_high, NN)
        )

    chunks = need // CHUNK
    image = lax.fori_loop(0, chunks, composite, jnp.zeros((WIDE, PIXELS), jnp.float32))
    errors[0:16, :] = jnp.zeros((16, PIXELS), jnp.float32)
    for k in range(3):
        part = image[16 + 16 * k : 32 + 16 * k, :]
        image_ref[k] = part
        errors[16 + 16 * k : 32 + 16 * k, :] = part - target_ref[k]

    def backward(step, later):
        later = list(later)
        chunk = chunks - 1 - step
        here = pl.ds(pl.multiple_of(chunk * CHUNK, CHUNK), CHUNK)
        colour_high, colour_low = split(rows[here, 0:WIDE])
        error_high, error_low = split(errors[...])
        powers[here, :] = (
            times(colour_low, error_high, NN)
            + times(colour_high, error_low, NN)
            + times(colour_high, error_high, NN)
        )
        for group in reversed(range(CHUNK // 8)):
            q = group % len(sets)
            part = pl.ds(pl.multiple_of(chunk * CHUNK + 8 * group, 8), 8)
            after = (chunk * (CHUNK // SEGMENTS) + group // len(sets) + 1).astype(jnp.float32)
            ends = jnp.where(rows[part, 7:8] == bases[q] + after, 1.0, 0.0)
            alpha = alphas[part, :]
            given = weights[part, :] * powers[part, :]
            rest = jnp.where(jnp.broadcast_to(ends, (8, PIXELS)) > 0.0, 0.0, later[q])
            ratio = alpha / (1.0 - alpha)
            alphas[part, :] = ratio
            powers[part, :] = given - ratio * rest
            later[q] = rest + given
        return tuple(later)

    later = lax.fori_loop(0, chunks, backward, tuple(zero for q in sets))
    carry = zero[0:1, :]
    behind = []
    for q in reversed(sets):
        final = pl.ds((span - 1) * SEGMENTS + 8 * q, 8)
        onward = jnp.where(rows[final, 7:8] > bases[q] + span, 1.0, 0.0) * (1.0 - seen[q])
        parts = []
        for k in reversed(range(8)):
            parts.append(carry)
            carry = later[q][k : k + 1, :] + onward[k : k + 1, :] * carry
        behind.append(jnp.concatenate(parts[::-1], axis=0))
    behind = behind[::-1]

    @pl.loop(0, chunks)
    def _(chunk):
        here = pl.ds(pl.multiple_of(chunk * CHUNK, CHUNK), CHUNK)
        for group in range(CHUNK // 8):
            q = group % len(sets)
            part = pl.ds(pl.multiple_of(chunk * CHUNK + 8 * group, 8), 8)
            tail = jnp.where(rows[part, 7:8] > bases[q] + span, 1.0, 0.0)
            rest = jnp.where(jnp.broadcast_to(tail, (8, PIXELS)) > 0.0, behind[q], 0.0)
            powers[part, :] = powers[part, :] - alphas[part, :] * rest
        power_high, power_low = split(powers[here, :])
        weight_high, weight_low = split(weights[here, :])
        error_high, error_low = split(errors[...])
        mono = mono_ref[...].astype(jnp.bfloat16)
        rows[here, 0:WIDE] = (
            times(power_low, mono, NT)
            + times(weight_low, error_high, NT)
            + times(weight_high, error_low, NT)
            + times(power_high, mono, NT)
            + times(weight_high, error_high, NT)
        )

    for segment in range(SEGMENTS):
        whole = slice(segment * span, segment * span + span)
        line[whole, :] = rows[pl.ds(segment, span, stride=SEGMENTS), :]

    def put(slot, start):
        count = counts_ref[slot]
        centre_x, centre_y = centre(slot)
        scale = jnp.where((lane < 6) | of_tile(slot), 1.0, 0.0)
        offset = jnp.where(lane == 11, centre_x, jnp.where(lane == 12, centre_y, 0.0))

        @pl.loop(0, (count + BATCH - 1) // BATCH)
        def _(step):
            first = step * BATCH
            picked = [line[pl.ds(start + first + part, 1), :] for part in range(BATCH)]
            for part in range(BATCH):
                place = lists_ref[slot, first + part]
                place = jnp.where(first + part < count, place, need)
                tab[pl.ds(place, 1), :] = picked[part] * scale + offset

        return start + count

    lax.fori_loop(0, slots, put, jnp.int32(0))
    sub = lax.broadcasted_iota(jnp.int32, (8, 128), 0)
    for block in range(need // 128):
        lanes = slice(block * 128, block * 128 + 128)
        values = tab[lanes, 0:WIDE].T
        low = values[8:16, :]
        for k in range(3):
            summed = jnp.sum(values[16 + 16 * k : 32 + 16 * k, :], axis=0, keepdims=True)
            low = jnp.where(sub == k, summed, low)
        first, second = packed(jnp.concatenate([values[0:8, :], low], axis=0))
        out_ref[2 * block] = first
        out_ref[2 * block + 1] = second


def render(features, tiles, lists, counts, active, target):
    need = features.shape[0] * HALF
    if target.shape[1] != 16 or need % (SEGMENTS * 128) != 0:
        raise ValueError("unsupported sizes")
    spot = np.arange(PIXELS)
    local_x = spot % TILE_SIDE + 0.5 - TILE_SIDE // 2
    local_y = spot // TILE_SIDE + 0.5 - TILE_SIDE // 2
    pixel = np.zeros((8, PIXELS), np.float32)
    pixel[0], pixel[1] = local_x, local_y
    mono = np.zeros((WIDE, PIXELS), np.float32)
    mono[0] = 1.0
    mono[1], mono[2] = local_x, local_y
    mono[3], mono[4], mono[5] = local_x * local_x, local_x * local_y, local_y * local_y
    smem = pl.BlockSpec(memory_space=pltpu.SMEM)
    vmem = pl.BlockSpec(memory_space=pltpu.VMEM)
    return pl.pallas_call(
        render_kernel,
        out_shape=(
            jax.ShapeDtypeStruct(target.shape, jnp.float32),
            jax.ShapeDtypeStruct(features.shape, jnp.float32),
        ),
        in_specs=[smem] * 4 + [vmem] * 4,
        out_specs=(vmem, vmem),
        scratch_shapes=[
            pltpu.VMEM((need + 8, 128), jnp.float32),
            pltpu.VMEM((need + BATCH, 128), jnp.float32),
            pltpu.VMEM((need, 128), jnp.float32),
            pltpu.VMEM((need, PIXELS), jnp.float32),
            pltpu.VMEM((need, PIXELS), jnp.float32),
            pltpu.VMEM((need, PIXELS), jnp.float32),
            pltpu.VMEM((WIDE, PIXELS), jnp.float32),
        ],
        compiler_params=pltpu.CompilerParams(vmem_limit_bytes=48 * 1024 * 1024),
        name="render",
    )(tiles, counts, active, lists, features, target, jnp.asarray(pixel), jnp.asarray(mono))


def per_device(
    sizes,
    gaussians,
    camera,
    fetch_index,
    tile_ids,
    tile_lists,
    tile_counts,
    tile_active,
    target,
):
    owned = gaussians.shape[1]
    need = fetch_index.shape[1]
    n = sizes[0] * sizes[1]
    if sizes[1] & (sizes[1] - 1) or n & (n - 1):
        raise ValueError("unsupported mesh")
    if need != n * HALF or owned % 1024 != 0:
        raise ValueError("unsupported sizes")
    smem = pl.BlockSpec(memory_space=pltpu.SMEM)
    vmem = pl.BlockSpec(memory_space=pltpu.VMEM)
    slabs = gaussians.reshape(59, owned // 128, 128)
    params = pltpu.CompilerParams(vmem_limit_bytes=40 * 1024 * 1024)
    me = lax.axis_index("tile") * sizes[1] + lax.axis_index("shard")
    shift = (lax.rem(me, 2) * HALF).astype(jnp.int32).reshape(1)
    features = pl.pallas_call(
        project_kernel,
        out_shape=jax.ShapeDtypeStruct((owned, 128), jnp.float32),
        in_specs=[smem, vmem],
        out_specs=vmem,
        scratch_shapes=[pltpu.VMEM((PACK, owned), jnp.float32)],
        compiler_params=params,
        name="project",
    )(camera, slabs)
    asked, table = pl.pallas_call(
        functools.partial(bring_kernel, sizes),
        out_shape=(
            jax.ShapeDtypeStruct((n, 1, 128), jnp.int32),
            jax.ShapeDtypeStruct((n, 8, 128), jnp.float32),
        ),
        in_specs=[vmem, vmem],
        out_specs=(vmem, vmem),
        scratch_shapes=[
            pltpu.SMEM((n, 1, 128), jnp.int32),
            pltpu.VMEM((128, 128), jnp.float32),
            pltpu.VMEM((n, 8, 128), jnp.float32),
        ]
        + [pltpu.SemaphoreType.DMA] * 5,
        compiler_params=pltpu.CompilerParams(
            collective_id=0, has_side_effects=True, vmem_limit_bytes=40 * 1024 * 1024
        ),
        name="bring",
    )(fetch_index.reshape(n // 2, 1, 128), features)
    asked = asked.reshape(n, 128)
    image, moments = render(
        table, tile_ids[0], tile_lists[0], tile_counts[0], tile_active[0], target
    )
    returned = exchange(moments, sizes, 2, "give")
    grads = pl.pallas_call(
        settle_kernel,
        out_shape=jax.ShapeDtypeStruct(slabs.shape, jnp.float32),
        in_specs=[smem, smem, smem, vmem, vmem],
        out_specs=vmem,
        scratch_shapes=[
            pltpu.VMEM((owned, 128), jnp.float32),
            pltpu.VMEM((128, 128), jnp.float32),
            pltpu.VMEM((PACK, owned), jnp.float32),
        ],
        compiler_params=params,
        name="settle",
    )(camera, asked, shift, slabs, returned)
    return (image, grads.reshape(gaussians.shape))


def solution(mesh):
    in_specs = (
        P(None, ("tile", "shard")),
        P(),
        P(("tile", "shard"), None),
        P(("tile", "shard"), None),
        P(("tile", "shard"), None, None),
        P(("tile", "shard"), None),
        P(("tile", "shard"), None),
        P(None, ("tile", "shard"), None),
    )
    out_specs = (P(None, ("tile", "shard"), None), P(None, ("tile", "shard")))
    sizes = (mesh.shape["tile"], mesh.shape["shard"])
    return jax.shard_map(
        functools.partial(per_device, sizes), mesh=mesh, in_specs=in_specs, out_specs=out_specs, check_vma=False
    )
```
